32 devices in a mesh: strike: 8 (over z, y), dip: 4 (over x, core).
Axes of the slice: x: 2, y: 2, z: 4, core: 2. Of those that a mesh axis runs over, the one named last changes fastest.
Arguments:
- slip_rate: float32 [3, 4096, 1024], P(None, 'strike', 'dip'), may hold values from -6 to 6
- history: bfloat16 [4, 3, 2, 1024, 4096], P(None, None, None, ('strike', 'dip')), may hold values from -6 to 6
- lengths: int32 [1024, 4096], P(('strike', 'dip')), may hold values from 1 to 4, as said below
- prestress: float32 [2, 4096, 1024], P(None, 'strike', 'dip'), may hold values from -8 to 8
- normal_stress: float32 [4096, 1024], P('strike', 'dip'), may hold values from 8 to 16
- direct_effect: float32 [4096, 1024], P('strike', 'dip'), may hold values from 0.01 to 0.04
- state_log: float32 [4096, 1024], P('strike', 'dip'), may hold values from 1 to 5
Outputs:
- next_rates: float32 [3, 4096, 1024], P(None, 'strike', 'dip')
- next_state: float32 [4096, 1024], P('strike', 'dip')
The draws below stay inside these ranges and needn't reach their ends.
Inputs may be any that keep to these rules, and one draw needn't show every extreme that they name: `lengths`: how many of the newest slip-rate spectra enter each wavenumber's stress transfer.
All inputs are finite; a program needn't handle non-finite values.
Results may differ from the reference program's by a relative error of at most 0.0003.
Values sent between devices are 32-bit elements; how exact they have to be, the bound alone decides.
A program may use at most 128 MiB of HBM per device.

```python
import math
import jax
import jax.numpy as jnp

NX = 4096
NZ = 1024
HIST = 4
NEWTON = 2


def draw_lengths(key, part):
    dip_modes = jnp.arange(NZ, dtype=jnp.int32)[:, None]
    strike_modes = jnp.arange(NX, dtype=jnp.int32)[None, :]
    dip_size = jnp.where(2 * dip_modes < NZ, dip_modes, NZ - dip_modes) * (NX // NZ)
    strike_size = jnp.where(2 * strike_modes < NX, strike_modes, NX - strike_modes)
    square = strike_size * strike_size + dip_size * dip_size
    radius = NX // 4 * (NX // 4)
    reach_count = jnp.ones((NZ, NX), jnp.int32)
    for multiple in range(1, HIST):
        reach_count = reach_count + (multiple * multiple * square <= radius).astype(jnp.int32)
    jitter = jax.random.randint(key, (NZ, NX), -1, 2, dtype=jnp.int32)
    drawn_lengths = jnp.clip(reach_count + jitter, 1, HIST)
    drawn_lengths = jnp.where(square == 0, HIST, drawn_lengths)
    farthest = (2 * strike_modes == NX) & (2 * dip_modes == NZ)
    return jnp.where(farthest, 1, drawn_lengths).astype(jnp.int32)


def steps_of(stream_key, shape, pieces, smallest, largest):
    factor_of = 1.0
    for position, blocks in pieces:
        heights = jax.random.uniform(jax.random.fold_in(jax.random.fold_in(stream_key, 6), position), (blocks,), jnp.float32, smallest / len(pieces), largest / len(pieces))
        factor_of = factor_of * jnp.repeat(jnp.exp(heights), shape[position] // blocks).reshape((-1,) + (1,) * (len(shape) - 1 - position))
    return factor_of


def bell_draw(key, shape, deviation, most, pieces=(), kind=jnp.bfloat16):
    factor_of = steps_of(key, shape, pieces, -0.22, 0.18) if pieces else 1.0
    values = jax.random.normal(key, shape, jnp.float32) * deviation * factor_of
    return jnp.minimum(jnp.maximum(values, -most), most).astype(kind)


def setup_inputs(seed: int = 0) -> dict:
    key_list = jax.random.split(jax.random.key(seed), 8)
    slip_rate = bell_draw(key_list[0], (3, NX, NZ), 1.0, 6.0, ((1, 8), (2, 4)), jnp.float32)
    history = bell_draw(key_list[1], (HIST, 3, 2, NZ, NX), 1.0, 6.0, ((3, 32),))
    lengths = draw_lengths(jax.random.fold_in(key_list[7], 71), 0)
    prestress = bell_draw(key_list[3], (2, NX, NZ), 2.0, 8.0, ((1, 8), (2, 4)), jnp.float32)
    normal_stress = jnp.clip(8.0 + 8.0 * jax.random.uniform(key_list[4], (NX, NZ), jnp.float32) ** steps_of(key_list[4], (NX, NZ), ((0, 8), (1, 4)), -0.2, 0.2), 8.0, 16.0)
    direct_effect = jnp.clip(jnp.exp(math.log(0.04) - 1.3862944 * jax.random.uniform(key_list[5], (NX, NZ), jnp.float32) ** steps_of(key_list[5], (NX, NZ), ((0, 8), (1, 4)), -0.2, 0.2)), 0.01, 0.04)
    state_log = jnp.clip(1.0 + 4.0 * jax.random.uniform(key_list[6], (NX, NZ), jnp.float32) ** steps_of(key_list[6], (NX, NZ), ((0, 8), (1, 4)), -0.2, 0.2), 1.0, 5.0)
    return dict(slip_rate=slip_rate, history=history, lengths=lengths, prestress=prestress, normal_stress=normal_stress, direct_effect=direct_effect, state_log=state_log)


time_step = 0.5
coupling = 0.5
decay_rate = 0.05
shear_speed = 0.6
opening_speed = 1.7
radiation = 0.5
healing = 1.0
slip_length = 2.0

def area_sine(ratio):
    return jnp.log(ratio + jnp.sqrt(ratio * ratio + 1.0))

def wave_geometry(dip_modes, strike_modes, dip_cells, strike_cells):
    signed_dip = jnp.where(2 * dip_modes < dip_cells, dip_modes, dip_modes - dip_cells)
    signed_strike = jnp.where(2 * strike_modes < strike_cells, strike_modes, strike_modes - strike_cells)
    wave_dip = signed_dip.astype(jnp.float32) * (2.0 * math.pi / dip_cells)
    wave_strike = signed_strike.astype(jnp.float32) * (2.0 * math.pi / strike_cells)
    modulus = jnp.sqrt(wave_strike * wave_strike + wave_dip * wave_dip)
    anchor = (signed_dip == 0) & (signed_strike == 0)
    safe_modulus = jnp.where(anchor, 1.0, modulus)
    unit_strike = jnp.where(anchor, 1.0, wave_strike / safe_modulus)
    unit_dip = jnp.where(anchor, 0.0, wave_dip / safe_modulus)
    return (modulus, unit_strike, unit_dip)

def delay_mixing(geometry, delay):
    modulus, unit_strike, unit_dip = geometry
    phase_arg = modulus * (time_step * (delay + 1.0))
    envelope = -coupling * time_step * modulus * jnp.exp(-decay_rate * phase_arg)
    mode_two = envelope * jnp.cos(phase_arg)
    mode_three = envelope * jnp.cos(shear_speed * phase_arg)
    mode_one = envelope * jnp.cos(opening_speed * phase_arg)
    mix_along = unit_strike * unit_strike * mode_two + unit_dip * unit_dip * mode_three
    mix_cross = unit_strike * unit_dip * (mode_two - mode_three)
    mix_across = unit_dip * unit_dip * mode_two + unit_strike * unit_strike * mode_three
    return (mix_along, mix_cross, mix_across, mode_one)

def delay_term(spectrum, mixing, active):
    mix_along, mix_cross, mix_across, mode_one = mixing
    force_strike = (mix_along * spectrum[0] + mix_cross * spectrum[1]) * active
    force_dip = (mix_cross * spectrum[0] + mix_across * spectrum[1]) * active
    force_open = mode_one * spectrum[2] * active
    return jnp.stack([force_strike, force_dip, force_open])

def friction_step(force_field, prestress, normal_stress, direct_effect, state_log):
    load_strike = prestress[0] + force_field[0]
    load_dip = prestress[1] + force_field[1]
    traction = jnp.sqrt(load_strike * load_strike + load_dip * load_dip)
    strength = direct_effect * normal_stress
    factor = 2.0 * radiation * jnp.exp(-state_log)
    estimate = jnp.minimum(traction / strength, area_sine(traction / factor))
    for repeat in range(NEWTON):
        residual = traction - strength * estimate - factor * jnp.sinh(estimate)
        estimate = estimate + residual / (strength + factor * jnp.cosh(estimate))
    slip_speed = (traction - strength * estimate) / radiation
    unit_scale = slip_speed / jnp.maximum(traction, 1.0)
    new_rates = jnp.stack([unit_scale * load_strike, unit_scale * load_dip, force_field[2] / radiation])
    new_state = state_log + time_step * (healing * jnp.exp(-state_log) - slip_speed / slip_length)
    return (new_rates, new_state)

def to_spectrum(space_field):
    complex_field = jnp.transpose(jnp.fft.fft2(space_field, norm='ortho'), (0, 2, 1))
    return jnp.stack([jnp.real(complex_field), jnp.imag(complex_field)], axis=1)

def to_field(spectrum):
    complex_field = jnp.transpose(spectrum[:, 0] + 1j * spectrum[:, 1], (0, 2, 1))
    return jnp.real(jnp.fft.ifft2(complex_field, norm='ortho'))

def transfer(recent, history, lengths, geometry):
    recent_count = len(recent)
    summed = jnp.zeros(recent[0].shape, jnp.float32)
    for offset in range(HIST):
        if offset < recent_count:
            source = recent[offset]
        else:
            source = history[offset - recent_count].astype(jnp.float32)
        active = (offset < lengths).astype(jnp.float32)
        summed = summed + delay_term(source, delay_mixing(geometry, float(offset)), active)
    return summed

def reference(slip_rate, history, lengths, prestress, normal_stress, direct_effect, state_log):
    dip_modes = jnp.arange(NZ, dtype=jnp.int32)[:, None]
    strike_modes = jnp.arange(NX, dtype=jnp.int32)[None, :]
    geometry = wave_geometry(dip_modes, strike_modes, NZ, NX)
    first_spec = to_spectrum(slip_rate)
    force_field = to_field(transfer([first_spec], history, lengths, geometry))
    next_rates, next_state = friction_step(force_field, prestress, normal_stress, direct_effect, state_log)
    second_spec = to_spectrum(next_rates)
    force_field = to_field(transfer([second_spec, first_spec], history, lengths, geometry))
    next_rates, next_state = friction_step(force_field, prestress, normal_stress, direct_effect, next_state)
    return (next_rates, next_state)
```

```python
import functools
import math

import jax
import jax.numpy as jnp
import numpy as np
from jax import lax
from jax.experimental import pallas as pl
from jax.experimental.pallas import tpu as pltpu
from jax.sharding import PartitionSpec as P

HIST = 4
NEWTON = 2


time_step = 0.5
coupling = 0.5
decay_rate = 0.05
shear_speed = 0.6
opening_speed = 1.7
radiation = 0.5
healing = 1.0
slip_length = 2.0
highest = lax.Precision.HIGHEST


def area_sine(ratio):
    return jnp.log(ratio + jnp.sqrt(ratio * ratio + 1.0))


def wave_geometry(dip_modes, strike_modes, dip_cells, strike_cells):
    signed_dip = jnp.where(2 * dip_modes < dip_cells, dip_modes, dip_modes - dip_cells)
    signed_strike = jnp.where(
        2 * strike_modes < strike_cells, strike_modes, strike_modes - strike_cells
    )
    wave_dip = signed_dip.astype(jnp.float32) * (2.0 * math.pi / dip_cells)
    wave_strike = signed_strike.astype(jnp.float32) * (2.0 * math.pi / strike_cells)
    modulus = jnp.sqrt(wave_strike * wave_strike + wave_dip * wave_dip)
    anchor = (signed_dip == 0) & (signed_strike == 0)
    safe_modulus = jnp.where(anchor, 1.0, modulus)
    unit_strike = jnp.where(anchor, 1.0, wave_strike / safe_modulus)
    unit_dip = jnp.where(anchor, 0.0, wave_dip / safe_modulus)
    return (modulus, unit_strike, unit_dip)


def delay_mixing(geometry, delay):
    modulus, unit_strike, unit_dip = geometry
    phase_arg = modulus * (time_step * (delay + 1.0))
    envelope = -coupling * time_step * modulus * jnp.exp(-decay_rate * phase_arg)
    mode_two = envelope * jnp.cos(phase_arg)
    mode_three = envelope * jnp.cos(shear_speed * phase_arg)
    mode_one = envelope * jnp.cos(opening_speed * phase_arg)
    mix_along = unit_strike * unit_strike * mode_two + unit_dip * unit_dip * mode_three
    mix_cross = unit_strike * unit_dip * (mode_two - mode_three)
    mix_across = unit_dip * unit_dip * mode_two + unit_strike * unit_strike * mode_three
    return (mix_along, mix_cross, mix_across, mode_one)


def delay_term(spectrum, mixing, active):
    mix_along, mix_cross, mix_across, mode_one = mixing
    force_strike = (mix_along * spectrum[0] + mix_cross * spectrum[1]) * active
    force_dip = (mix_cross * spectrum[0] + mix_across * spectrum[1]) * active
    force_open = mode_one * spectrum[2] * active
    return jnp.stack([force_strike, force_dip, force_open])


def friction_step(force_field, prestress, normal_stress, direct_effect, state_log):
    load_strike = prestress[0] + force_field[0]
    load_dip = prestress[1] + force_field[1]
    traction = jnp.sqrt(load_strike * load_strike + load_dip * load_dip)
    strength = direct_effect * normal_stress
    factor = 2.0 * radiation * jnp.exp(-state_log)
    estimate = jnp.minimum(traction / strength, area_sine(traction / factor))
    for repeat in range(NEWTON):
        residual = traction - strength * estimate - factor * jnp.sinh(estimate)
        estimate = estimate + residual / (strength + factor * jnp.cosh(estimate))
    slip_speed = (traction - strength * estimate) / radiation
    unit_scale = slip_speed / jnp.maximum(traction, 1.0)
    new_rates = jnp.stack(
        [unit_scale * load_strike, unit_scale * load_dip, force_field[2] / radiation]
    )
    new_state = state_log + time_step * (healing * jnp.exp(-state_log) - slip_speed / slip_length)
    return (new_rates, new_state)


def phase_table(first_index, second_index, period):
    turn_count = first_index[:, None] * second_index[None, :] % period
    angle_table = turn_count.astype(jnp.float32) * (2.0 * math.pi / period)
    return (jnp.cos(angle_table), jnp.sin(angle_table))


def contract(pattern, first_operand, second_operand):
    return jnp.einsum(pattern, first_operand, second_operand, precision=highest)


def pair_section(part_real, part_imag, pattern, cos_table, sin_table, sign):
    out_real = contract(pattern, part_real, cos_table) - sign * contract(
        pattern, part_imag, sin_table
    )
    out_imag = contract(pattern, part_imag, cos_table) + sign * contract(
        pattern, part_real, sin_table
    )
    return (out_real, out_imag)


def twist_phase(part_real, part_imag, cos_table, sin_table, sign):
    out_real = cos_table * part_real - sign * sin_table * part_imag
    out_imag = cos_table * part_imag + sign * sin_table * part_real
    return (out_real, out_imag)


def shards(slip_rate, history, lengths, prestress, normal_stress, direct_effect, state_log):
    strike_count = lax.axis_size("strike")
    dip_count = lax.axis_size("dip")
    strike_index = lax.axis_index("strike")
    dip_index = lax.axis_index("dip")
    row_count = slip_rate.shape[1]
    dip_block = slip_rate.shape[2]
    mode_rows = history.shape[3]
    strike_cells = history.shape[4]
    dip_cells = dip_block * dip_count
    unit_modes = dip_count * mode_rows
    quarter_rows = row_count // dip_count
    norm_dip = 1.0 / math.sqrt(dip_cells)
    norm_strike = 1.0 / math.sqrt(strike_cells)
    local_modes = jnp.arange(mode_rows, dtype=jnp.int32)
    dip_modes = (strike_index * dip_count + dip_index) * mode_rows + local_modes
    strike_modes = jnp.arange(strike_cells, dtype=jnp.int32)
    geometry = wave_geometry(dip_modes[:, None], strike_modes[None, :], dip_cells, strike_cells)
    coarse_all = jnp.arange(unit_modes, dtype=jnp.int32)
    coarse_own = dip_index * mode_rows + local_modes
    outer_index = jnp.arange(strike_count, dtype=jnp.int32)
    inner_index = jnp.arange(row_count, dtype=jnp.int32)
    cos_outer, sin_outer = phase_table(outer_index, outer_index, strike_count)
    cos_bend, sin_bend = phase_table(outer_index, inner_index, strike_cells)
    cos_bend = cos_bend * norm_strike
    sin_bend = sin_bend * norm_strike
    cos_inner, sin_inner = phase_table(inner_index, inner_index, row_count)

    def strike_forward(spectral):
        item_count = spectral.shape[0]
        grid_view = spectral.reshape(item_count, 2, mode_rows, strike_count, row_count)
        section_real, section_imag = pair_section(
            grid_view[:, 0], grid_view[:, 1], "ngpr,kp->ngkr", cos_outer, sin_outer, -1.0
        )
        bent_real, bent_imag = twist_phase(section_real, section_imag, cos_bend, sin_bend, -1.0)
        out_real, out_imag = pair_section(
            bent_real, bent_imag, "ngkr,rm->ngmk", cos_inner, sin_inner, -1.0
        )
        return jnp.stack([out_real, out_imag], axis=1).reshape(
            item_count, 2, mode_rows, strike_cells
        )

    def strike_inverse(spectral):
        grid_view = spectral.reshape(3, 2, mode_rows, row_count, strike_count)
        section_real, section_imag = pair_section(
            grid_view[:, 0], grid_view[:, 1], "ngmk,rm->ngrk", cos_inner, sin_inner, 1.0
        )
        bent_real, bent_imag = twist_phase(section_real, section_imag, cos_bend.T, sin_bend.T, 1.0)
        out_real, out_imag = pair_section(
            bent_real, bent_imag, "ngrk,kp->ngpr", cos_outer, sin_outer, 1.0
        )
        return jnp.stack([out_real, out_imag], axis=1).reshape(3, 2, mode_rows, strike_cells)

    def to_modes(space_field):
        gathered = lax.all_gather(space_field, "dip", axis=2, tiled=True)
        cos_first, sin_first = phase_table(coarse_all, coarse_own, unit_modes)
        cos_twist, sin_twist = phase_table(outer_index, coarse_own, dip_cells)
        grid_view = gathered.reshape(3, row_count, unit_modes, strike_count)
        first_real = contract("cxab,au->cxbu", grid_view, cos_first)
        first_imag = -contract("cxab,au->cxbu", grid_view, sin_first)
        bent_real, bent_imag = twist_phase(
            first_real, first_imag, cos_twist * norm_dip, sin_twist * norm_dip, -1.0
        )
        out_real, out_imag = pair_section(
            bent_real, bent_imag, "cxbi,bs->csix", cos_outer, sin_outer, -1.0
        )
        dip_spec = jnp.stack([out_real, out_imag], axis=1).reshape(3, 2, dip_block, row_count)
        return strike_forward(
            lax.all_to_all(dip_spec, "strike", split_axis=2, concat_axis=3, tiled=True)
        )

    def to_space(mode_field):
        mixed_rows = strike_inverse(mode_field)
        sectioned = mixed_rows.reshape(3, 2, mode_rows, strike_count, dip_count * quarter_rows)
        back = lax.all_to_all(
            lax.all_to_all(sectioned, "strike", split_axis=3, concat_axis=2, tiled=True),
            "dip",
            split_axis=4,
            concat_axis=2,
            tiled=True,
        )
        grid_view = back.reshape(3, 2, dip_count, strike_count, mode_rows, quarter_rows)
        cos_last, sin_last = phase_table(coarse_all, coarse_all, unit_modes)
        first_real, first_imag = pair_section(
            grid_view[:, 0], grid_view[:, 1], "cdsix,bs->cxbdi", cos_outer, sin_outer, 1.0
        )
        first_real = first_real.reshape(3, quarter_rows, strike_count, unit_modes)
        first_imag = first_imag.reshape(3, quarter_rows, strike_count, unit_modes)
        cos_twist, sin_twist = phase_table(outer_index, coarse_all, dip_cells)
        bent_real, bent_imag = twist_phase(
            first_real, first_imag, cos_twist * norm_dip, sin_twist * norm_dip, 1.0
        )
        space_part = contract("cxbu,au->cxab", bent_real, cos_last) - contract(
            "cxbu,au->cxab", bent_imag, sin_last
        )
        space_rows = space_part.reshape(3, quarter_rows, dip_cells)
        return lax.all_to_all(space_rows, "dip", split_axis=2, concat_axis=1, tiled=True)

    def transfer(recent):
        recent_count = len(recent)
        summed = jnp.zeros(recent[0].shape, jnp.float32)
        for offset in range(HIST):
            if offset < recent_count:
                source = recent[offset]
            else:
                source = history[offset - recent_count].astype(jnp.float32)
            active = (offset < lengths).astype(jnp.float32)
            summed = summed + delay_term(source, delay_mixing(geometry, float(offset)), active)
        return summed

    first_spec = to_modes(slip_rate)
    force_field = to_space(transfer([first_spec]))
    next_rates, next_state = friction_step(
        force_field, prestress, normal_stress, direct_effect, state_log
    )
    second_spec = to_modes(next_rates)
    force_field = to_space(transfer([second_spec, first_spec]))
    next_rates, next_state = friction_step(
        force_field, prestress, normal_stress, direct_effect, next_state
    )
    return (next_rates, next_state)


LANES = 128
SUBLANES = 8


def turn(part_real, part_imag, count, index, sign):
    index = index % count
    if index == 0:
        return part_real, part_imag
    if 2 * index == count:
        return -part_real, -part_imag
    if 4 * index == count:
        return (-part_imag, part_real) if sign > 0 else (part_imag, -part_real)
    angle = sign * 2.0 * math.pi * index / count
    cosine, sine = math.cos(angle), math.sin(angle)
    if 8 * index == count:
        return (
            cosine * (part_real - part_imag) if sign > 0 else cosine * (part_real + part_imag),
            cosine * (part_imag + part_real) if sign > 0 else cosine * (part_imag - part_real),
        )
    return (
        cosine * part_real - sine * part_imag,
        cosine * part_imag + sine * part_real,
    )


def butterfly(reals, imags, sign):
    count = len(reals)
    if count == 1:
        return reals, imags
    even_real, even_imag = butterfly(reals[0::2], imags[0::2], sign)
    odd_real, odd_imag = butterfly(reals[1::2], imags[1::2], sign)
    top, low = [], []
    for index in range(count // 2):
        bent_real, bent_imag = turn(odd_real[index], odd_imag[index], count, index, sign)
        top.append((even_real[index] + bent_real, even_imag[index] + bent_imag))
        low.append((even_real[index] - bent_real, even_imag[index] - bent_imag))
    both = top + low
    return [item[0] for item in both], [item[1] for item in both]


def split_product(left, high, low):
    left_high = left.astype(jnp.bfloat16)
    left_low = (left - left_high.astype(jnp.float32)).astype(jnp.bfloat16)
    dot = functools.partial(jnp.dot, preferred_element_type=jnp.float32)
    return dot(left_high, high) + (dot(left_low, high) + dot(left_high, low))


def owner_kernel(keep, *refs):
    if keep:
        x_ref, mix_ref, add_ref, later_mix_ref, later_ref, bend_ref, high_ref, low_ref = refs[:8]
        out_ref, later_out_ref, line, spec = refs[8:]
    else:
        x_ref, mix_ref, add_ref, bend_ref, high_ref, low_ref = refs[:6]
        out_ref, line, spec = refs[6:]
    blocks = x_ref.shape[0]
    rows = blocks * SUBLANES
    width = 2 * LANES
    halves = (slice(0, LANES), slice(LANES, width))
    for comp in range(3):
        own = slice(comp * LANES, (comp + 1) * LANES)
        reals, imags = butterfly(
            [x_ref[block, 0, :, own] for block in range(blocks)],
            [x_ref[block, 1, :, own] for block in range(blocks)],
            -1,
        )
        for mode in range(blocks):
            cosine = bend_ref[0, pl.ds(mode, 1), :]
            sine = bend_ref[1, pl.ds(mode, 1), :]
            line[comp, mode, :, halves[0]] = reals[mode] * cosine + imags[mode] * sine
            line[comp, mode, :, halves[1]] = imags[mode] * cosine - reals[mode] * sine
        spec[comp] = split_product(
            line[comp].reshape(rows, width), high_ref[0], low_ref[0]
        ).reshape(blocks, SUBLANES, width)
    for half in halves:
        along, across, opening = (spec[comp, :, :, half] for comp in range(3))
        line[0, :, :, half] = mix_ref[0] * along + mix_ref[1] * across + add_ref[0, :, :, half]
        line[1, :, :, half] = mix_ref[1] * along + mix_ref[2] * across + add_ref[1, :, :, half]
        line[2, :, :, half] = mix_ref[3] * opening + add_ref[2, :, :, half]
        if keep:
            later_out_ref[0, :, :, half] = (
                later_mix_ref[0] * along + later_mix_ref[1] * across + later_ref[0, :, :, half]
            )
            later_out_ref[1, :, :, half] = (
                later_mix_ref[1] * along + later_mix_ref[2] * across + later_ref[1, :, :, half]
            )
            later_out_ref[2, :, :, half] = later_mix_ref[3] * opening + later_ref[2, :, :, half]
    for comp in range(3):
        own = slice(comp * LANES, (comp + 1) * LANES)
        spec[comp] = split_product(
            line[comp].reshape(rows, width), high_ref[1], low_ref[1]
        ).reshape(blocks, SUBLANES, width)
        reals, imags = [], []
        for mode in range(blocks):
            cosine = bend_ref[0, pl.ds(mode, 1), :]
            sine = bend_ref[1, pl.ds(mode, 1), :]
            real, imag = spec[comp, mode, :, halves[0]], spec[comp, mode, :, halves[1]]
            reals.append(real * cosine - imag * sine)
            imags.append(imag * cosine + real * sine)
        reals, imags = butterfly(reals, imags, 1)
        for block in range(blocks):
            out_ref[block, 0, :, own] = reals[block]
            out_ref[block, 1, :, own] = imags[block]


def strike_pass(arrived, mixing, addend, tables, later=None):
    blocks, _, modes, depth = arrived.shape
    bend, high, low = tables
    tiles = modes // SUBLANES
    wide = pl.BlockSpec((blocks, 2, SUBLANES, depth), lambda tile: (0, 0, tile, 0))
    factors = pl.BlockSpec((4, blocks, SUBLANES, LANES), lambda tile: (0, 0, tile, 0))
    field = pl.BlockSpec((3, blocks, SUBLANES, 2 * LANES), lambda tile: (0, 0, tile, 0))
    fixed = [
        pl.BlockSpec(item.shape, lambda tile, rank=item.ndim: (0,) * rank) for item in tables
    ]
    operands = [arrived, mixing, addend]
    in_specs = [wide, factors, field]
    out_specs = [wide]
    out_shape = [jax.ShapeDtypeStruct(arrived.shape, jnp.float32)]
    if later is not None:
        operands += list(later)
        in_specs += [factors, field]
        out_specs.append(field)
        out_shape.append(jax.ShapeDtypeStruct(addend.shape, jnp.float32))
    return pl.pallas_call(
        functools.partial(owner_kernel, later is not None),
        grid=(tiles,),
        in_specs=in_specs + fixed,
        out_specs=out_specs,
        out_shape=out_shape,
        scratch_shapes=[
            pltpu.VMEM((3, blocks, SUBLANES, 2 * LANES), jnp.float32),
            pltpu.VMEM((3, blocks, SUBLANES, 2 * LANES), jnp.float32),
        ],
        compiler_params=pltpu.CompilerParams(vmem_limit_bytes=40 * 1024 * 1024),
        cost_estimate=pl.CostEstimate(
            flops=12 * arrived.size * 2 * LANES, bytes_accessed=16 * arrived.size, transcendentals=0
        ),
    )(*operands, bend, high, low)


def halves_of(table):
    table = table.astype(np.float32)
    high = table.astype(jnp.bfloat16)
    return high, (table - high.astype(np.float32)).astype(jnp.bfloat16)


def strike_tables(blocks, strike_cells):
    first, second = np.arange(blocks)[:, None], np.arange(LANES)[None, :]
    angle = 2.0 * np.pi * (first * second % strike_cells) / strike_cells
    bend = np.stack([np.cos(angle), np.sin(angle)]) / math.sqrt(strike_cells)
    line = np.arange(LANES)
    angle = 2.0 * np.pi * (line[:, None] * line[None, :] % LANES) / LANES
    cosine, sine = np.cos(angle), np.sin(angle)
    forward = np.block([[cosine, -sine], [sine, cosine]])
    inverse = np.block([[cosine, sine], [-sine, cosine]])
    high, low = halves_of(np.stack([forward, inverse]))
    return jnp.asarray(bend, jnp.float32), jnp.asarray(high), jnp.asarray(low)


def dip_table(devices, dip_cells):
    modes = np.arange(dip_cells)
    angle = 2.0 * np.pi * (modes[:, None] * modes[None, :] % dip_cells) / dip_cells
    pair = np.stack([np.cos(angle), -np.sin(angle)]) / math.sqrt(dip_cells)
    pair = pair.reshape(2, devices, dip_cells // devices, dip_cells).transpose(1, 0, 2, 3)
    return jnp.asarray(pair.reshape(2 * dip_cells, dip_cells), jnp.float32)


def all_mixing(geometry):
    modulus, unit_strike, unit_dip = geometry
    base = modulus * time_step
    decay = jnp.exp(-decay_rate * base)
    speeds = (1.0, shear_speed, opening_speed)
    one = [jnp.cos(speed * base) for speed in speeds]
    last, now = [1.0, 1.0, 1.0], list(one)
    envelope = -coupling * time_step * modulus
    square_strike, square_dip = unit_strike * unit_strike, unit_dip * unit_dip
    cross = unit_strike * unit_dip
    factors = []
    for _ in range(HIST):
        envelope = envelope * decay
        two, three, opening = (envelope * value for value in now)
        factors.append(
            (
                square_strike * two + square_dip * three,
                cross * (two - three),
                square_dip * two + square_strike * three,
                opening,
            )
        )
        last, now = now, [2.0 * a * b - c for a, b, c in zip(one, now, last)]
    return factors


def fast_shards(slip_rate, history, lengths, prestress, normal_stress, direct_effect, state_log):
    strike_count = lax.axis_size("strike")
    dip_count = lax.axis_size("dip")
    devices = strike_count * dip_count
    row_count = slip_rate.shape[1]
    dip_cells = slip_rate.shape[2] * dip_count
    modes = history.shape[3]
    strike_cells = history.shape[4]
    rows = row_count // dip_count
    own = lax.axis_index("strike") * dip_count + lax.axis_index("dip")
    table = dip_table(devices, dip_cells)
    tables = strike_tables(devices, strike_cells)
    local_modes = own * modes + jnp.arange(modes, dtype=jnp.int32)
    strike_modes = jnp.arange(strike_cells, dtype=jnp.int32)
    precise = lax.Precision.HIGH

    def send(space_field):
        spread = lax.all_to_all(space_field, "dip", split_axis=1, concat_axis=2, tiled=True)
        dip_spec = jnp.einsum(
            "kz,xz->kx", table, spread.reshape(3 * rows, dip_cells), precision=precise
        )
        moved = lax.all_to_all(
            dip_spec, ("strike", "dip"), split_axis=0, concat_axis=0, tiled=True
        )
        return moved.reshape(devices, 2, modes, 3 * rows)

    def receive(strike_rows):
        moved = lax.all_to_all(
            strike_rows.reshape(2 * dip_cells, 3 * rows),
            ("strike", "dip"),
            split_axis=0,
            concat_axis=0,
            tiled=True,
        )
        space_rows = jnp.einsum("kx,kz->xz", moved, table, precision=precise)
        return lax.all_to_all(
            space_rows.reshape(3, rows, dip_cells), "dip", split_axis=2, concat_axis=1, tiled=True
        )

    def by_residue(plain):
        lead = plain.shape[:-1]
        return plain.reshape(lead + (rows, devices))

    residue = jnp.arange(devices, dtype=jnp.int32)[:, None, None]
    step = jnp.arange(rows, dtype=jnp.int32)[None, None, :]
    sorted_mixing = all_mixing(
        wave_geometry(local_modes[None, :, None], residue + devices * step, dip_cells, strike_cells)
    )
    reach = jnp.transpose(by_residue(lengths), (2, 0, 1))
    mixing = jnp.stack(sorted_mixing[0])
    later_mixing = jnp.stack(sorted_mixing[1]) * (1 < reach).astype(jnp.float32)
    plain_mixing = all_mixing(
        wave_geometry(local_modes[:, None], strike_modes[None, :], dip_cells, strike_cells)
    )

    def past(first):
        summed = 0.0
        for offset in range(first, HIST):
            active = (offset < lengths).astype(jnp.float32)
            source = history[offset - first].astype(jnp.float32)
            summed = summed + delay_term(source, plain_mixing[offset], active)
        summed = jnp.transpose(by_residue(summed), (0, 4, 2, 1, 3))
        return summed.reshape(3, devices, modes, 2 * rows)

    arrived = send(slip_rate)
    strike_rows, addend = strike_pass(
        arrived, mixing, past(1), tables, (later_mixing, past(2))
    )
    next_rates, next_state = friction_step(
        receive(strike_rows), prestress, normal_stress, direct_effect, state_log
    )
    (strike_rows,) = strike_pass(send(next_rates), mixing, addend, tables)
    return friction_step(
        receive(strike_rows), prestress, normal_stress, direct_effect, next_state
    )


def choose(slip_rate, history, *others):
    devices = lax.axis_size("strike") * lax.axis_size("dip")
    fits = (
        history.shape[4] == devices * LANES
        and history.shape[3] % SUBLANES == 0
        and devices & (devices - 1) == 0
    )
    return (fast_shards if fits else shards)(slip_rate, history, *others)


def solution(mesh):
    return jax.shard_map(
        choose,
        mesh=mesh,
        in_specs=(
            P(None, "strike", "dip"),
            P(None, None, None, ("strike", "dip"), None),
            P(("strike", "dip"), None),
            P(None, "strike", "dip"),
            P("strike", "dip"),
            P("strike", "dip"),
            P("strike", "dip"),
        ),
        out_specs=(P(None, "strike", "dip"), P("strike", "dip")),
        check_vma=False,
    )
```

```python
import functools
import math

import jax
import jax.numpy as jnp
import numpy as np
from jax import lax
from jax.experimental import pallas as pl
from jax.experimental.pallas import tpu as pltpu
from jax.sharding import PartitionSpec as P

HIST = 4
NEWTON = 2


time_step = 0.5
coupling = 0.5
decay_rate = 0.05
shear_speed = 0.6
opening_speed = 1.7
radiation = 0.5
healing = 1.0
slip_length = 2.0
highest = lax.Precision.HIGHEST


def area_sine(ratio):
    return jnp.log(ratio + jnp.sqrt(ratio * ratio + 1.0))


def wave_geometry(dip_modes, strike_modes, dip_cells, strike_cells):
    signed_dip = jnp.where(2 * dip_modes < dip_cells, dip_modes, dip_modes - dip_cells)
    signed_strike = jnp.where(
        2 * strike_modes < strike_cells, strike_modes, strike_modes - strike_cells
    )
    wave_dip = signed_dip.astype(jnp.float32) * (2.0 * math.pi / dip_cells)
    wave_strike = signed_strike.astype(jnp.float32) * (2.0 * math.pi / strike_cells)
    modulus = jnp.sqrt(wave_strike * wave_strike + wave_dip * wave_dip)
    anchor = (signed_dip == 0) & (signed_strike == 0)
    safe_modulus = jnp.where(anchor, 1.0, modulus)
    unit_strike = jnp.where(anchor, 1.0, wave_strike / safe_modulus)
    unit_dip = jnp.where(anchor, 0.0, wave_dip / safe_modulus)
    return (modulus, unit_strike, unit_dip)


def delay_mixing(geometry, delay):
    modulus, unit_strike, unit_dip = geometry
    phase_arg = modulus * (time_step * (delay + 1.0))
    envelope = -coupling * time_step * modulus * jnp.exp(-decay_rate * phase_arg)
    mode_two = envelope * jnp.cos(phase_arg)
    mode_three = envelope * jnp.cos(shear_speed * phase_arg)
    mode_one = envelope * jnp.cos(opening_speed * phase_arg)
    mix_along = unit_strike * unit_strike * mode_two + unit_dip * unit_dip * mode_three
    mix_cross = unit_strike * unit_dip * (mode_two - mode_three)
    mix_across = unit_dip * unit_dip * mode_two + unit_strike * unit_strike * mode_three
    return (mix_along, mix_cross, mix_across, mode_one)


def delay_term(spectrum, mixing, active):
    mix_along, mix_cross, mix_across, mode_one = mixing
    force_strike = (mix_along * spectrum[0] + mix_cross * spectrum[1]) * active
    force_dip = (mix_cross * spectrum[0] + mix_across * spectrum[1]) * active
    force_open = mode_one * spectrum[2] * active
    return jnp.stack([force_strike, force_dip, force_open])


def friction_planes(force_field, prestress, strength, state_log):
    load_strike = prestress[0] + force_field[0]
    load_dip = prestress[1] + force_field[1]
    traction = jnp.sqrt(load_strike * load_strike + load_dip * load_dip)
    factor = 2.0 * radiation * jnp.exp(-state_log)
    estimate = jnp.minimum(traction / strength, area_sine(traction / factor))
    for repeat in range(NEWTON):
        residual = traction - strength * estimate - factor * jnp.sinh(estimate)
        estimate = estimate + residual / (strength + factor * jnp.cosh(estimate))
    slip_speed = (traction - strength * estimate) / radiation
    unit_scale = slip_speed / jnp.maximum(traction, 1.0)
    new_rates = [unit_scale * load_strike, unit_scale * load_dip, force_field[2] / radiation]
    new_state = state_log + time_step * (healing * jnp.exp(-state_log) - slip_speed / slip_length)
    return (new_rates, new_state)


def friction_step(force_field, prestress, normal_stress, direct_effect, state_log):
    new_rates, new_state = friction_planes(
        force_field, prestress, direct_effect * normal_stress, state_log
    )
    return (jnp.stack(new_rates), new_state)


def phase_table(first_index, second_index, period):
    turn_count = first_index[:, None] * second_index[None, :] % period
    angle_table = turn_count.astype(jnp.float32) * (2.0 * math.pi / period)
    return (jnp.cos(angle_table), jnp.sin(angle_table))


def contract(pattern, first_operand, second_operand):
    return jnp.einsum(pattern, first_operand, second_operand, precision=highest)


def pair_section(part_real, part_imag, pattern, cos_table, sin_table, sign):
    out_real = contract(pattern, part_real, cos_table) - sign * contract(
        pattern, part_imag, sin_table
    )
    out_imag = contract(pattern, part_imag, cos_table) + sign * contract(
        pattern, part_real, sin_table
    )
    return (out_real, out_imag)


def twist_phase(part_real, part_imag, cos_table, sin_table, sign):
    out_real = cos_table * part_real - sign * sin_table * part_imag
    out_imag = cos_table * part_imag + sign * sin_table * part_real
    return (out_real, out_imag)


def shards(slip_rate, history, lengths, prestress, normal_stress, direct_effect, state_log):
    strike_count = lax.axis_size("strike")
    dip_count = lax.axis_size("dip")
    strike_index = lax.axis_index("strike")
    dip_index = lax.axis_index("dip")
    row_count = slip_rate.shape[1]
    dip_block = slip_rate.shape[2]
    mode_rows = history.shape[3]
    strike_cells = history.shape[4]
    dip_cells = dip_block * dip_count
    unit_modes = dip_count * mode_rows
    quarter_rows = row_count // dip_count
    norm_dip = 1.0 / math.sqrt(dip_cells)
    norm_strike = 1.0 / math.sqrt(strike_cells)
    local_modes = jnp.arange(mode_rows, dtype=jnp.int32)
    dip_modes = (strike_index * dip_count + dip_index) * mode_rows + local_modes
    strike_modes = jnp.arange(strike_cells, dtype=jnp.int32)
    geometry = wave_geometry(dip_modes[:, None], strike_modes[None, :], dip_cells, strike_cells)
    coarse_all = jnp.arange(unit_modes, dtype=jnp.int32)
    coarse_own = dip_index * mode_rows + local_modes
    outer_index = jnp.arange(strike_count, dtype=jnp.int32)
    inner_index = jnp.arange(row_count, dtype=jnp.int32)
    cos_outer, sin_outer = phase_table(outer_index, outer_index, strike_count)
    cos_bend, sin_bend = phase_table(outer_index, inner_index, strike_cells)
    cos_bend = cos_bend * norm_strike
    sin_bend = sin_bend * norm_strike
    cos_inner, sin_inner = phase_table(inner_index, inner_index, row_count)

    def strike_forward(spectral):
        item_count = spectral.shape[0]
        grid_view = spectral.reshape(item_count, 2, mode_rows, strike_count, row_count)
        section_real, section_imag = pair_section(
            grid_view[:, 0], grid_view[:, 1], "ngpr,kp->ngkr", cos_outer, sin_outer, -1.0
        )
        bent_real, bent_imag = twist_phase(section_real, section_imag, cos_bend, sin_bend, -1.0)
        out_real, out_imag = pair_section(
            bent_real, bent_imag, "ngkr,rm->ngmk", cos_inner, sin_inner, -1.0
        )
        return jnp.stack([out_real, out_imag], axis=1).reshape(
            item_count, 2, mode_rows, strike_cells
        )

    def strike_inverse(spectral):
        grid_view = spectral.reshape(3, 2, mode_rows, row_count, strike_count)
        section_real, section_imag = pair_section(
            grid_view[:, 0], grid_view[:, 1], "ngmk,rm->ngrk", cos_inner, sin_inner, 1.0
        )
        bent_real, bent_imag = twist_phase(section_real, section_imag, cos_bend.T, sin_bend.T, 1.0)
        out_real, out_imag = pair_section(
            bent_real, bent_imag, "ngrk,kp->ngpr", cos_outer, sin_outer, 1.0
        )
        return jnp.stack([out_real, out_imag], axis=1).reshape(3, 2, mode_rows, strike_cells)

    def to_modes(space_field):
        gathered = lax.all_gather(space_field, "dip", axis=2, tiled=True)
        cos_first, sin_first = phase_table(coarse_all, coarse_own, unit_modes)
        cos_twist, sin_twist = phase_table(outer_index, coarse_own, dip_cells)
        grid_view = gathered.reshape(3, row_count, unit_modes, strike_count)
        first_real = contract("cxab,au->cxbu", grid_view, cos_first)
        first_imag = -contract("cxab,au->cxbu", grid_view, sin_first)
        bent_real, bent_imag = twist_phase(
            first_real, first_imag, cos_twist * norm_dip, sin_twist * norm_dip, -1.0
        )
        out_real, out_imag = pair_section(
            bent_real, bent_imag, "cxbi,bs->csix", cos_outer, sin_outer, -1.0
        )
        dip_spec = jnp.stack([out_real, out_imag], axis=1).reshape(3, 2, dip_block, row_count)
        return strike_forward(
            lax.all_to_all(dip_spec, "strike", split_axis=2, concat_axis=3, tiled=True)
        )

    def to_space(mode_field):
        mixed_rows = strike_inverse(mode_field)
        sectioned = mixed_rows.reshape(3, 2, mode_rows, strike_count, dip_count * quarter_rows)
        back = lax.all_to_all(
            lax.all_to_all(sectioned, "strike", split_axis=3, concat_axis=2, tiled=True),
            "dip",
            split_axis=4,
            concat_axis=2,
            tiled=True,
        )
        grid_view = back.reshape(3, 2, dip_count, strike_count, mode_rows, quarter_rows)
        cos_last, sin_last = phase_table(coarse_all, coarse_all, unit_modes)
        first_real, first_imag = pair_section(
            grid_view[:, 0], grid_view[:, 1], "cdsix,bs->cxbdi", cos_outer, sin_outer, 1.0
        )
        first_real = first_real.reshape(3, quarter_rows, strike_count, unit_modes)
        first_imag = first_imag.reshape(3, quarter_rows, strike_count, unit_modes)
        cos_twist, sin_twist = phase_table(outer_index, coarse_all, dip_cells)
        bent_real, bent_imag = twist_phase(
            first_real, first_imag, cos_twist * norm_dip, sin_twist * norm_dip, 1.0
        )
        space_part = contract("cxbu,au->cxab", bent_real, cos_last) - contract(
            "cxbu,au->cxab", bent_imag, sin_last
        )
        space_rows = space_part.reshape(3, quarter_rows, dip_cells)
        return lax.all_to_all(space_rows, "dip", split_axis=2, concat_axis=1, tiled=True)

    def transfer(recent):
        recent_count = len(recent)
        summed = jnp.zeros(recent[0].shape, jnp.float32)
        for offset in range(HIST):
            if offset < recent_count:
                source = recent[offset]
            else:
                source = history[offset - recent_count].astype(jnp.float32)
            active = (offset < lengths).astype(jnp.float32)
            summed = summed + delay_term(source, delay_mixing(geometry, float(offset)), active)
        return summed

    first_spec = to_modes(slip_rate)
    force_field = to_space(transfer([first_spec]))
    next_rates, next_state = friction_step(
        force_field, prestress, normal_stress, direct_effect, state_log
    )
    second_spec = to_modes(next_rates)
    force_field = to_space(transfer([second_spec, first_spec]))
    next_rates, next_state = friction_step(
        force_field, prestress, normal_stress, direct_effect, next_state
    )
    return (next_rates, next_state)


LANES = 128
SUBLANES = 8


def turn(part_real, part_imag, count, index, sign):
    index = index % count
    if index == 0:
        return part_real, part_imag
    if 2 * index == count:
        return -part_real, -part_imag
    if 4 * index == count:
        return (-part_imag, part_real) if sign > 0 else (part_imag, -part_real)
    angle = sign * 2.0 * math.pi * index / count
    cosine, sine = math.cos(angle), math.sin(angle)
    if 8 * index == count:
        return (
            cosine * (part_real - part_imag) if sign > 0 else cosine * (part_real + part_imag),
            cosine * (part_imag + part_real) if sign > 0 else cosine * (part_imag - part_real),
        )
    return (
        cosine * part_real - sine * part_imag,
        cosine * part_imag + sine * part_real,
    )


def butterfly(reals, imags, sign):
    count = len(reals)
    if count == 1:
        return reals, imags
    even_real, even_imag = butterfly(reals[0::2], imags[0::2], sign)
    odd_real, odd_imag = butterfly(reals[1::2], imags[1::2], sign)
    top, low = [], []
    for index in range(count // 2):
        bent_real, bent_imag = turn(odd_real[index], odd_imag[index], count, index, sign)
        top.append((even_real[index] + bent_real, even_imag[index] + bent_imag))
        low.append((even_real[index] - bent_real, even_imag[index] - bent_imag))
    both = top + low
    return [item[0] for item in both], [item[1] for item in both]


def split_product(left, high, low):
    left_high = left.astype(jnp.bfloat16)
    left_low = (left - left_high.astype(jnp.float32)).astype(jnp.bfloat16)
    dot = functools.partial(jnp.dot, preferred_element_type=jnp.float32)
    return dot(left_high, high) + (dot(left_low, high) + dot(left_high, low))


def owner_kernel(keep, *refs):
    if keep:
        x_ref, mix_ref, add_ref, later_mix_ref, later_ref, bend_ref, high_ref, low_ref = refs[:8]
        out_ref, later_out_ref, line, spec = refs[8:]
    else:
        x_ref, mix_ref, add_ref, bend_ref, high_ref, low_ref = refs[:6]
        out_ref, line, spec = refs[6:]
    blocks = x_ref.shape[0]
    rows = blocks * SUBLANES
    width = 2 * LANES
    halves = (slice(0, LANES), slice(LANES, width))
    for comp in range(3):
        own = slice(comp * LANES, (comp + 1) * LANES)
        reals, imags = butterfly(
            [x_ref[block, 0, :, own] for block in range(blocks)],
            [x_ref[block, 1, :, own] for block in range(blocks)],
            -1,
        )
        for mode in range(blocks):
            cosine = bend_ref[0, pl.ds(mode, 1), :]
            sine = bend_ref[1, pl.ds(mode, 1), :]
            line[comp, mode, :, halves[0]] = reals[mode] * cosine + imags[mode] * sine
            line[comp, mode, :, halves[1]] = imags[mode] * cosine - reals[mode] * sine
        spec[comp] = split_product(
            line[comp].reshape(rows, width), high_ref[0], low_ref[0]
        ).reshape(blocks, SUBLANES, width)
    for part, half in enumerate(halves):
        along, across, opening = (spec[comp, :, :, half] for comp in range(3))
        line[0, :, :, half] = mix_ref[0] * along + mix_ref[1] * across + add_ref[0, part]
        line[1, :, :, half] = mix_ref[1] * along + mix_ref[2] * across + add_ref[1, part]
        line[2, :, :, half] = mix_ref[3] * opening + add_ref[2, part]
        if keep:
            later_out_ref[0, part] = (
                later_mix_ref[0] * along + later_mix_ref[1] * across + later_ref[0, part]
            )
            later_out_ref[1, part] = (
                later_mix_ref[1] * along + later_mix_ref[2] * across + later_ref[1, part]
            )
            later_out_ref[2, part] = later_mix_ref[3] * opening + later_ref[2, part]
    for comp in range(3):
        own = slice(comp * LANES, (comp + 1) * LANES)
        spec[comp] = split_product(
            line[comp].reshape(rows, width), high_ref[1], low_ref[1]
        ).reshape(blocks, SUBLANES, width)
        reals, imags = [], []
        for mode in range(blocks):
            cosine = bend_ref[0, pl.ds(mode, 1), :]
            sine = bend_ref[1, pl.ds(mode, 1), :]
            real, imag = spec[comp, mode, :, halves[0]], spec[comp, mode, :, halves[1]]
            reals.append(real * cosine - imag * sine)
            imags.append(imag * cosine + real * sine)
        reals, imags = butterfly(reals, imags, 1)
        for block in range(blocks):
            out_ref[block, 0, :, own] = reals[block]
            out_ref[block, 1, :, own] = imags[block]


def strike_pass(arrived, mixing, addend, tables, later=None):
    blocks, _, modes, depth = arrived.shape
    bend, high, low = tables
    tiles = modes // SUBLANES
    wide = pl.BlockSpec((blocks, 2, SUBLANES, depth), lambda tile: (0, 0, tile, 0))
    factors = pl.BlockSpec((4, blocks, SUBLANES, LANES), lambda tile: (0, 0, tile, 0))
    field = pl.BlockSpec((3, 2, blocks, SUBLANES, LANES), lambda tile: (0, 0, 0, tile, 0))
    fixed = [
        pl.BlockSpec(item.shape, lambda tile, rank=item.ndim: (0,) * rank) for item in tables
    ]
    operands = [arrived, mixing, addend]
    in_specs = [wide, factors, field]
    out_specs = [wide]
    out_shape = [jax.ShapeDtypeStruct(arrived.shape, jnp.float32)]
    if later is not None:
        operands += list(later)
        in_specs += [factors, field]
        out_specs.append(field)
        out_shape.append(jax.ShapeDtypeStruct(addend.shape, jnp.float32))
    return pl.pallas_call(
        functools.partial(owner_kernel, later is not None),
        grid=(tiles,),
        in_specs=in_specs + fixed,
        out_specs=out_specs,
        out_shape=out_shape,
        scratch_shapes=[
            pltpu.VMEM((3, blocks, SUBLANES, 2 * LANES), jnp.float32),
            pltpu.VMEM((3, blocks, SUBLANES, 2 * LANES), jnp.float32),
        ],
        compiler_params=pltpu.CompilerParams(vmem_limit_bytes=40 * 1024 * 1024),
        cost_estimate=pl.CostEstimate(
            flops=12 * arrived.size * 2 * LANES, bytes_accessed=16 * arrived.size, transcendentals=0
        ),
    )(*operands, bend, high, low)


def halves_of(table):
    table = table.astype(np.float32)
    high = table.astype(jnp.bfloat16)
    return high, (table - high.astype(np.float32)).astype(jnp.bfloat16)


def strike_tables(blocks, strike_cells):
    first, second = np.arange(blocks)[:, None], np.arange(LANES)[None, :]
    angle = 2.0 * np.pi * (first * second % strike_cells) / strike_cells
    bend = np.stack([np.cos(angle), np.sin(angle)]) / math.sqrt(strike_cells)
    line = np.arange(LANES)
    angle = 2.0 * np.pi * (line[:, None] * line[None, :] % LANES) / LANES
    cosine, sine = np.cos(angle), np.sin(angle)
    forward = np.block([[cosine, -sine], [sine, cosine]])
    inverse = np.block([[cosine, sine], [-sine, cosine]])
    high, low = halves_of(np.stack([forward, inverse]))
    return jnp.asarray(bend, jnp.float32), jnp.asarray(high), jnp.asarray(low)


def dip_tables(devices, dip_cells):
    modes = np.arange(dip_cells)
    angle = 2.0 * np.pi * (modes[:, None] * modes[None, :] % dip_cells) / dip_cells
    pair = np.stack([np.cos(angle), -np.sin(angle)]) / math.sqrt(dip_cells)
    pair = pair.reshape(2, devices, dip_cells // devices, dip_cells).transpose(1, 0, 2, 3)
    pair = pair.reshape(2 * dip_cells, dip_cells)
    return jnp.asarray(pair, jnp.float32), jnp.asarray(pair.T, jnp.float32)


def all_mixing(geometry):
    modulus, unit_strike, unit_dip = geometry
    base = modulus * time_step
    decay = jnp.exp(-decay_rate * base)
    speeds = (1.0, shear_speed, opening_speed)
    one = [jnp.cos(speed * base) for speed in speeds]
    last, now = [1.0, 1.0, 1.0], list(one)
    envelope = -coupling * time_step * modulus
    square_strike, square_dip = unit_strike * unit_strike, unit_dip * unit_dip
    cross = unit_strike * unit_dip
    factors = []
    for _ in range(HIST):
        envelope = envelope * decay
        two, three, opening = (envelope * value for value in now)
        factors.append(
            (
                square_strike * two + square_dip * three,
                cross * (two - three),
                square_dip * two + square_strike * three,
                opening,
            )
        )
        last, now = now, [2.0 * a * b - c for a, b, c in zip(one, now, last)]
    return factors


def fast_shards(slip_rate, history, lengths, prestress, normal_stress, direct_effect, state_log):
    strike_count = lax.axis_size("strike")
    dip_count = lax.axis_size("dip")
    devices = strike_count * dip_count
    row_count = slip_rate.shape[1]
    dip_cells = slip_rate.shape[2] * dip_count
    modes = history.shape[3]
    strike_cells = history.shape[4]
    rows = row_count // dip_count
    own = lax.axis_index("strike") * dip_count + lax.axis_index("dip")
    table, back_table = dip_tables(devices, dip_cells)
    tables = strike_tables(devices, strike_cells)
    local_modes = own * modes + jnp.arange(modes, dtype=jnp.int32)
    strike_modes = jnp.arange(strike_cells, dtype=jnp.int32)
    precise = lax.Precision.HIGH

    def to_rows(planes):
        count = planes.shape[0]
        parts = planes.reshape(count, dip_count, rows, -1)
        parts = jnp.transpose(parts, (1, 3, 0, 2)).reshape(dip_count, -1, count * rows)
        moved = lax.all_to_all(parts, "dip", split_axis=0, concat_axis=0, tiled=True)
        return moved.reshape(dip_cells, count * rows)

    def from_rows(space_rows):
        count = space_rows.shape[1] // rows
        parts = space_rows.reshape(dip_count, -1, count * rows)
        moved = lax.all_to_all(parts, "dip", split_axis=0, concat_axis=0, tiled=True)
        moved = moved.reshape(dip_count, -1, count, rows)
        return jnp.transpose(moved, (2, 0, 3, 1)).reshape(count, row_count, -1)

    def send(space_rows):
        dip_spec = jnp.dot(table, space_rows, precision=precise)
        moved = lax.all_to_all(
            dip_spec, ("strike", "dip"), split_axis=0, concat_axis=0, tiled=True
        )
        return moved.reshape(devices, 2, modes, 3 * rows)

    def receive(strike_rows):
        moved = lax.all_to_all(
            strike_rows.reshape(2 * dip_cells, 3 * rows),
            ("strike", "dip"),
            split_axis=0,
            concat_axis=0,
            tiled=True,
        )
        return planes_of(jnp.dot(back_table, moved, precision=precise))

    def planes_of(space_rows):
        return [
            space_rows[:, start : start + rows] for start in range(0, space_rows.shape[1], rows)
        ]

    def by_residue(plain):
        lead = plain.shape[:-1]
        return plain.reshape(lead + (rows, devices))

    residue = jnp.arange(devices, dtype=jnp.int32)[:, None, None]
    step = jnp.arange(rows, dtype=jnp.int32)[None, None, :]
    sorted_mixing = all_mixing(
        wave_geometry(local_modes[None, :, None], residue + devices * step, dip_cells, strike_cells)
    )
    reach = jnp.transpose(by_residue(lengths), (2, 0, 1))
    mixing = jnp.stack(sorted_mixing[0])
    later_mixing = jnp.stack(sorted_mixing[1]) * (1 < reach).astype(jnp.float32)
    plain_mixing = all_mixing(
        wave_geometry(local_modes[:, None], strike_modes[None, :], dip_cells, strike_cells)
    )

    def past(first):
        strike_sum, dip_sum, open_sum = 0.0, 0.0, 0.0
        for offset in range(first, HIST):
            along, cross, across, opening = plain_mixing[offset]
            active = (offset < lengths).astype(jnp.float32)
            source = history[offset - first].astype(jnp.float32)
            strike_sum += (along * source[0] + cross * source[1]) * active
            dip_sum += (cross * source[0] + across * source[1]) * active
            open_sum += opening * source[2] * active
        summed = jnp.stack([strike_sum, dip_sum, open_sum])
        return jnp.transpose(by_residue(summed), (0, 1, 4, 2, 3))

    arrived = send(to_rows(slip_rate))
    load = jnp.concatenate(
        [prestress, (direct_effect * normal_stress)[None], state_log[None]]
    )
    load_strike, load_dip, strength, state = planes_of(to_rows(load))
    strike_rows, addend = strike_pass(
        arrived, mixing, past(1), tables, (later_mixing, past(2))
    )
    rates, state = friction_planes(receive(strike_rows), (load_strike, load_dip), strength, state)
    (strike_rows,) = strike_pass(send(jnp.concatenate(rates, axis=1)), mixing, addend, tables)
    rates, state = friction_planes(receive(strike_rows), (load_strike, load_dip), strength, state)
    result = from_rows(jnp.concatenate(rates + [state], axis=1))
    return (result[:3], result[3])


def choose(slip_rate, history, *others):
    devices = lax.axis_size("strike") * lax.axis_size("dip")
    fits = (
        history.shape[4] == devices * LANES
        and history.shape[3] % SUBLANES == 0
        and devices & (devices - 1) == 0
    )
    return (fast_shards if fits else shards)(slip_rate, history, *others)


def solution(mesh):
    return jax.shard_map(
        choose,
        mesh=mesh,
        in_specs=(
            P(None, "strike", "dip"),
            P(None, None, None, ("strike", "dip"), None),
            P(("strike", "dip"), None),
            P(None, "strike", "dip"),
            P("strike", "dip"),
            P("strike", "dip"),
            P("strike", "dip"),
        ),
        out_specs=(P(None, "strike", "dip"), P("strike", "dip")),
        check_vma=False,
    )
```

```python
import functools
import math

import jax
import jax.numpy as jnp
import numpy as np
from jax import lax
from jax.experimental import pallas as pl
from jax.experimental.pallas import tpu as pltpu
from jax.sharding import PartitionSpec as P

HIST = 4
NEWTON = 2


time_step = 0.5
coupling = 0.5
decay_rate = 0.05
shear_speed = 0.6
opening_speed = 1.7
radiation = 0.5
healing = 1.0
slip_length = 2.0
highest = lax.Precision.HIGHEST


def area_sine(ratio):
    return jnp.log(ratio + jnp.sqrt(ratio * ratio + 1.0))


def wave_geometry(dip_modes, strike_modes, dip_cells, strike_cells):
    signed_dip = jnp.where(2 * dip_modes < dip_cells, dip_modes, dip_modes - dip_cells)
    signed_strike = jnp.where(
        2 * strike_modes < strike_cells, strike_modes, strike_modes - strike_cells
    )
    wave_dip = signed_dip.astype(jnp.float32) * (2.0 * math.pi / dip_cells)
    wave_strike = signed_strike.astype(jnp.float32) * (2.0 * math.pi / strike_cells)
    modulus = jnp.sqrt(wave_strike * wave_strike + wave_dip * wave_dip)
    anchor = (signed_dip == 0) & (signed_strike == 0)
    safe_modulus = jnp.where(anchor, 1.0, modulus)
    unit_strike = jnp.where(anchor, 1.0, wave_strike / safe_modulus)
    unit_dip = jnp.where(anchor, 0.0, wave_dip / safe_modulus)
    return (modulus, unit_strike, unit_dip)


def delay_mixing(geometry, delay):
    modulus, unit_strike, unit_dip = geometry
    phase_arg = modulus * (time_step * (delay + 1.0))
    envelope = -coupling * time_step * modulus * jnp.exp(-decay_rate * phase_arg)
    mode_two = envelope * jnp.cos(phase_arg)
    mode_three = envelope * jnp.cos(shear_speed * phase_arg)
    mode_one = envelope * jnp.cos(opening_speed * phase_arg)
    mix_along = unit_strike * unit_strike * mode_two + unit_dip * unit_dip * mode_three
    mix_cross = unit_strike * unit_dip * (mode_two - mode_three)
    mix_across = unit_dip * unit_dip * mode_two + unit_strike * unit_strike * mode_three
    return (mix_along, mix_cross, mix_across, mode_one)


def delay_term(spectrum, mixing, active):
    mix_along, mix_cross, mix_across, mode_one = mixing
    force_strike = (mix_along * spectrum[0] + mix_cross * spectrum[1]) * active
    force_dip = (mix_cross * spectrum[0] + mix_across * spectrum[1]) * active
    force_open = mode_one * spectrum[2] * active
    return jnp.stack([force_strike, force_dip, force_open])


def friction_planes(force_field, prestress, strength, state_log):
    load_strike = prestress[0] + force_field[0]
    load_dip = prestress[1] + force_field[1]
    traction = jnp.sqrt(load_strike * load_strike + load_dip * load_dip)
    factor = 2.0 * radiation * jnp.exp(-state_log)
    estimate = jnp.minimum(traction / strength, area_sine(traction / factor))
    for repeat in range(NEWTON):
        residual = traction - strength * estimate - factor * jnp.sinh(estimate)
        estimate = estimate + residual / (strength + factor * jnp.cosh(estimate))
    slip_speed = (traction - strength * estimate) / radiation
    unit_scale = slip_speed / jnp.maximum(traction, 1.0)
    new_rates = [unit_scale * load_strike, unit_scale * load_dip]
    new_state = state_log + time_step * (healing * jnp.exp(-state_log) - slip_speed / slip_length)
    return (new_rates, new_state)


def friction_step(force_field, prestress, normal_stress, direct_effect, state_log):
    new_rates, new_state = friction_planes(
        force_field, prestress, direct_effect * normal_stress, state_log
    )
    return (jnp.stack(new_rates + [force_field[2] / radiation]), new_state)


def phase_table(first_index, second_index, period):
    turn_count = first_index[:, None] * second_index[None, :] % period
    angle_table = turn_count.astype(jnp.float32) * (2.0 * math.pi / period)
    return (jnp.cos(angle_table), jnp.sin(angle_table))


def contract(pattern, first_operand, second_operand):
    return jnp.einsum(pattern, first_operand, second_operand, precision=highest)


def pair_section(part_real, part_imag, pattern, cos_table, sin_table, sign):
    out_real = contract(pattern, part_real, cos_table) - sign * contract(
        pattern, part_imag, sin_table
    )
    out_imag = contract(pattern, part_imag, cos_table) + sign * contract(
        pattern, part_real, sin_table
    )
    return (out_real, out_imag)


def twist_phase(part_real, part_imag, cos_table, sin_table, sign):
    out_real = cos_table * part_real - sign * sin_table * part_imag
    out_imag = cos_table * part_imag + sign * sin_table * part_real
    return (out_real, out_imag)


def shards(slip_rate, history, lengths, prestress, normal_stress, direct_effect, state_log):
    strike_count = lax.axis_size("strike")
    dip_count = lax.axis_size("dip")
    strike_index = lax.axis_index("strike")
    dip_index = lax.axis_index("dip")
    row_count = slip_rate.shape[1]
    dip_block = slip_rate.shape[2]
    mode_rows = history.shape[3]
    strike_cells = history.shape[4]
    dip_cells = dip_block * dip_count
    unit_modes = dip_count * mode_rows
    quarter_rows = row_count // dip_count
    norm_dip = 1.0 / math.sqrt(dip_cells)
    norm_strike = 1.0 / math.sqrt(strike_cells)
    local_modes = jnp.arange(mode_rows, dtype=jnp.int32)
    dip_modes = (strike_index * dip_count + dip_index) * mode_rows + local_modes
    strike_modes = jnp.arange(strike_cells, dtype=jnp.int32)
    geometry = wave_geometry(dip_modes[:, None], strike_modes[None, :], dip_cells, strike_cells)
    coarse_all = jnp.arange(unit_modes, dtype=jnp.int32)
    coarse_own = dip_index * mode_rows + local_modes
    outer_index = jnp.arange(strike_count, dtype=jnp.int32)
    inner_index = jnp.arange(row_count, dtype=jnp.int32)
    cos_outer, sin_outer = phase_table(outer_index, outer_index, strike_count)
    cos_bend, sin_bend = phase_table(outer_index, inner_index, strike_cells)
    cos_bend = cos_bend * norm_strike
    sin_bend = sin_bend * norm_strike
    cos_inner, sin_inner = phase_table(inner_index, inner_index, row_count)

    def strike_forward(spectral):
        item_count = spectral.shape[0]
        grid_view = spectral.reshape(item_count, 2, mode_rows, strike_count, row_count)
        section_real, section_imag = pair_section(
            grid_view[:, 0], grid_view[:, 1], "ngpr,kp->ngkr", cos_outer, sin_outer, -1.0
        )
        bent_real, bent_imag = twist_phase(section_real, section_imag, cos_bend, sin_bend, -1.0)
        out_real, out_imag = pair_section(
            bent_real, bent_imag, "ngkr,rm->ngmk", cos_inner, sin_inner, -1.0
        )
        return jnp.stack([out_real, out_imag], axis=1).reshape(
            item_count, 2, mode_rows, strike_cells
        )

    def strike_inverse(spectral):
        grid_view = spectral.reshape(3, 2, mode_rows, row_count, strike_count)
        section_real, section_imag = pair_section(
            grid_view[:, 0], grid_view[:, 1], "ngmk,rm->ngrk", cos_inner, sin_inner, 1.0
        )
        bent_real, bent_imag = twist_phase(section_real, section_imag, cos_bend.T, sin_bend.T, 1.0)
        out_real, out_imag = pair_section(
            bent_real, bent_imag, "ngrk,kp->ngpr", cos_outer, sin_outer, 1.0
        )
        return jnp.stack([out_real, out_imag], axis=1).reshape(3, 2, mode_rows, strike_cells)

    def to_modes(space_field):
        gathered = lax.all_gather(space_field, "dip", axis=2, tiled=True)
        cos_first, sin_first = phase_table(coarse_all, coarse_own, unit_modes)
        cos_twist, sin_twist = phase_table(outer_index, coarse_own, dip_cells)
        grid_view = gathered.reshape(3, row_count, unit_modes, strike_count)
        first_real = contract("cxab,au->cxbu", grid_view, cos_first)
        first_imag = -contract("cxab,au->cxbu", grid_view, sin_first)
        bent_real, bent_imag = twist_phase(
            first_real, first_imag, cos_twist * norm_dip, sin_twist * norm_dip, -1.0
        )
        out_real, out_imag = pair_section(
            bent_real, bent_imag, "cxbi,bs->csix", cos_outer, sin_outer, -1.0
        )
        dip_spec = jnp.stack([out_real, out_imag], axis=1).reshape(3, 2, dip_block, row_count)
        return strike_forward(
            lax.all_to_all(dip_spec, "strike", split_axis=2, concat_axis=3, tiled=True)
        )

    def to_space(mode_field):
        mixed_rows = strike_inverse(mode_field)
        sectioned = mixed_rows.reshape(3, 2, mode_rows, strike_count, dip_count * quarter_rows)
        back = lax.all_to_all(
            lax.all_to_all(sectioned, "strike", split_axis=3, concat_axis=2, tiled=True),
            "dip",
            split_axis=4,
            concat_axis=2,
            tiled=True,
        )
        grid_view = back.reshape(3, 2, dip_count, strike_count, mode_rows, quarter_rows)
        cos_last, sin_last = phase_table(coarse_all, coarse_all, unit_modes)
        first_real, first_imag = pair_section(
            grid_view[:, 0], grid_view[:, 1], "cdsix,bs->cxbdi", cos_outer, sin_outer, 1.0
        )
        first_real = first_real.reshape(3, quarter_rows, strike_count, unit_modes)
        first_imag = first_imag.reshape(3, quarter_rows, strike_count, unit_modes)
        cos_twist, sin_twist = phase_table(outer_index, coarse_all, dip_cells)
        bent_real, bent_imag = twist_phase(
            first_real, first_imag, cos_twist * norm_dip, sin_twist * norm_dip, 1.0
        )
        space_part = contract("cxbu,au->cxab", bent_real, cos_last) - contract(
            "cxbu,au->cxab", bent_imag, sin_last
        )
        space_rows = space_part.reshape(3, quarter_rows, dip_cells)
        return lax.all_to_all(space_rows, "dip", split_axis=2, concat_axis=1, tiled=True)

    def transfer(recent):
        recent_count = len(recent)
        summed = jnp.zeros(recent[0].shape, jnp.float32)
        for offset in range(HIST):
            if offset < recent_count:
                source = recent[offset]
            else:
                source = history[offset - recent_count].astype(jnp.float32)
            active = (offset < lengths).astype(jnp.float32)
            summed = summed + delay_term(source, delay_mixing(geometry, float(offset)), active)
        return summed

    first_spec = to_modes(slip_rate)
    force_field = to_space(transfer([first_spec]))
    next_rates, next_state = friction_step(
        force_field, prestress, normal_stress, direct_effect, state_log
    )
    second_spec = to_modes(next_rates)
    force_field = to_space(transfer([second_spec, first_spec]))
    next_rates, next_state = friction_step(
        force_field, prestress, normal_stress, direct_effect, next_state
    )
    return (next_rates, next_state)


LANES = 128
SUBLANES = 8


def turn(part_real, part_imag, count, index, sign):
    index = index % count
    if index == 0:
        return part_real, part_imag
    if 2 * index == count:
        return -part_real, -part_imag
    if 4 * index == count:
        return (-part_imag, part_real) if sign > 0 else (part_imag, -part_real)
    angle = sign * 2.0 * math.pi * index / count
    cosine, sine = math.cos(angle), math.sin(angle)
    if 8 * index == count:
        return (
            cosine * (part_real - part_imag) if sign > 0 else cosine * (part_real + part_imag),
            cosine * (part_imag + part_real) if sign > 0 else cosine * (part_imag - part_real),
        )
    return (
        cosine * part_real - sine * part_imag,
        cosine * part_imag + sine * part_real,
    )


def butterfly(reals, imags, sign):
    count = len(reals)
    if count == 1:
        return reals, imags
    even_real, even_imag = butterfly(reals[0::2], imags[0::2], sign)
    odd_real, odd_imag = butterfly(reals[1::2], imags[1::2], sign)
    top, low = [], []
    for index in range(count // 2):
        bent_real, bent_imag = turn(odd_real[index], odd_imag[index], count, index, sign)
        top.append((even_real[index] + bent_real, even_imag[index] + bent_imag))
        low.append((even_real[index] - bent_real, even_imag[index] - bent_imag))
    both = top + low
    return [item[0] for item in both], [item[1] for item in both]


def split_product(left, high, low):
    left_high = left.astype(jnp.bfloat16)
    left_low = (left - left_high.astype(jnp.float32)).astype(jnp.bfloat16)
    dot = functools.partial(jnp.dot, preferred_element_type=jnp.float32)
    return dot(left_high, high) + (dot(left_low, high) + dot(left_high, low))


def owner_kernel(comps, keep, past, *refs):
    x_ref, mix_ref, add_ref = refs[:3]
    refs = refs[3:]
    if past:
        past_mix_ref, past_ref = refs[:2]
        refs = refs[2:]
    bend_ref, high_ref, low_ref, out_ref = refs[:4]
    line, spec = refs[-2:]
    blocks = x_ref.shape[0]
    rows = blocks * SUBLANES
    width = 2 * LANES
    halves = (slice(0, LANES), slice(LANES, width))
    for comp in range(comps):
        own = slice(comp * LANES, (comp + 1) * LANES)
        reals, imags = butterfly(
            [x_ref[block, 0, :, own] for block in range(blocks)],
            [x_ref[block, 1, :, own] for block in range(blocks)],
            -1,
        )
        for mode in range(blocks):
            cosine = bend_ref[0, pl.ds(mode, 1), :]
            sine = bend_ref[1, pl.ds(mode, 1), :]
            line[comp, mode, :, halves[0]] = reals[mode] * cosine + imags[mode] * sine
            line[comp, mode, :, halves[1]] = imags[mode] * cosine - reals[mode] * sine
        spec[comp] = split_product(
            line[comp].reshape(rows, width), high_ref[0], low_ref[0]
        ).reshape(blocks, SUBLANES, width)
    for part, half in enumerate(halves):
        if comps == 1:
            line[0, :, :, half] = mix_ref[0] * spec[0, :, :, half] + add_ref[0, part]
            continue
        along, across = spec[0, :, :, half], spec[1, :, :, half]
        strike_sum = mix_ref[0] * along + mix_ref[1] * across + add_ref[0, part]
        dip_sum = mix_ref[1] * along + mix_ref[2] * across + add_ref[1, part]
        if past:
            strike_sum += past_mix_ref[0] * past_ref[0, part] + past_mix_ref[1] * past_ref[1, part]
            dip_sum += past_mix_ref[1] * past_ref[0, part] + past_mix_ref[2] * past_ref[1, part]
        line[0, :, :, half] = strike_sum
        line[1, :, :, half] = dip_sum
        if keep:
            refs[4][0, part] = along
            refs[4][1, part] = across
    for comp in range(comps):
        own = slice(comp * LANES, (comp + 1) * LANES)
        spec[comp] = split_product(
            line[comp].reshape(rows, width), high_ref[1], low_ref[1]
        ).reshape(blocks, SUBLANES, width)
        reals, imags = [], []
        for mode in range(blocks):
            cosine = bend_ref[0, pl.ds(mode, 1), :]
            sine = bend_ref[1, pl.ds(mode, 1), :]
            real, imag = spec[comp, mode, :, halves[0]], spec[comp, mode, :, halves[1]]
            reals.append(real * cosine - imag * sine)
            imags.append(imag * cosine + real * sine)
        reals, imags = butterfly(reals, imags, 1)
        for block in range(blocks):
            out_ref[block, 0, :, own] = reals[block]
            out_ref[block, 1, :, own] = imags[block]


def strike_pass(arrived, mixing, addend, tables, past=(), keep=False):
    blocks, _, modes, depth = arrived.shape
    comps = depth // LANES
    wide = pl.BlockSpec((blocks, 2, SUBLANES, depth), lambda tile: (0, 0, tile, 0))
    factors = pl.BlockSpec(
        (mixing.shape[0], blocks, SUBLANES, LANES), lambda tile: (0, 0, tile, 0)
    )
    field = pl.BlockSpec((comps, 2, blocks, SUBLANES, LANES), lambda tile: (0, 0, 0, tile, 0))
    fixed = [
        pl.BlockSpec(item.shape, lambda tile, rank=item.ndim: (0,) * rank) for item in tables
    ]
    out_shape = [jax.ShapeDtypeStruct(arrived.shape, jnp.float32)]
    if keep:
        out_shape.append(jax.ShapeDtypeStruct(addend.shape, jnp.float32))
    return pl.pallas_call(
        functools.partial(owner_kernel, comps, keep, bool(past)),
        grid=(modes // SUBLANES,),
        in_specs=[wide, factors, field] + [factors, field][: len(past)] + fixed,
        out_specs=[wide, field][: len(out_shape)],
        out_shape=out_shape,
        scratch_shapes=[
            pltpu.VMEM((comps, blocks, SUBLANES, 2 * LANES), jnp.float32),
            pltpu.VMEM((comps, blocks, SUBLANES, 2 * LANES), jnp.float32),
        ],
        compiler_params=pltpu.CompilerParams(vmem_limit_bytes=40 * 1024 * 1024),
        cost_estimate=pl.CostEstimate(
            flops=12 * arrived.size * 2 * LANES, bytes_accessed=16 * arrived.size, transcendentals=0
        ),
    )(arrived, mixing, addend, *past, *tables)


def halves_of(table):
    table = table.astype(np.float32)
    high = table.astype(jnp.bfloat16)
    return high, (table - high.astype(np.float32)).astype(jnp.bfloat16)


def strike_tables(blocks, strike_cells):
    first, second = np.arange(blocks)[:, None], np.arange(LANES)[None, :]
    angle = 2.0 * np.pi * (first * second % strike_cells) / strike_cells
    bend = np.stack([np.cos(angle), np.sin(angle)]) / math.sqrt(strike_cells)
    line = np.arange(LANES)
    angle = 2.0 * np.pi * (line[:, None] * line[None, :] % LANES) / LANES
    cosine, sine = np.cos(angle), np.sin(angle)
    forward = np.block([[cosine, -sine], [sine, cosine]])
    inverse = np.block([[cosine, sine], [-sine, cosine]])
    high, low = halves_of(np.stack([forward, inverse]))
    return jnp.asarray(bend, jnp.float32), jnp.asarray(high), jnp.asarray(low)


def dip_tables(devices, dip_cells):
    modes = np.arange(dip_cells)
    angle = 2.0 * np.pi * (modes[:, None] * modes[None, :] % dip_cells) / dip_cells
    pair = np.stack([np.cos(angle), -np.sin(angle)]) / math.sqrt(dip_cells)
    pair = pair.reshape(2, devices, dip_cells // devices, dip_cells).transpose(1, 0, 2, 3)
    pair = pair.reshape(2 * dip_cells, dip_cells)
    return jnp.asarray(pair, jnp.float32), jnp.asarray(pair.T, jnp.float32)


def all_mixing(geometry):
    modulus, unit_strike, unit_dip = geometry
    base = modulus * time_step
    decay = jnp.exp(-decay_rate * base)
    speeds = (1.0, shear_speed, opening_speed)
    one = [jnp.cos(speed * base) for speed in speeds]
    last, now = [1.0, 1.0, 1.0], list(one)
    envelope = -coupling * time_step * modulus
    square_strike, square_dip = unit_strike * unit_strike, unit_dip * unit_dip
    cross = unit_strike * unit_dip
    factors = []
    for _ in range(HIST):
        envelope = envelope * decay
        two, three, opening = (envelope * value for value in now)
        factors.append(
            (
                square_strike * two + square_dip * three,
                cross * (two - three),
                square_dip * two + square_strike * three,
                opening,
            )
        )
        last, now = now, [2.0 * a * b - c for a, b, c in zip(one, now, last)]
    return factors


def fast_shards(slip_rate, history, lengths, prestress, normal_stress, direct_effect, state_log):
    strike_count = lax.axis_size("strike")
    dip_count = lax.axis_size("dip")
    devices = strike_count * dip_count
    row_count = slip_rate.shape[1]
    dip_cells = slip_rate.shape[2] * dip_count
    modes = history.shape[3]
    strike_cells = history.shape[4]
    rows = row_count // dip_count
    own = lax.axis_index("strike") * dip_count + lax.axis_index("dip")
    table, back_table = dip_tables(devices, dip_cells)
    tables = strike_tables(devices, strike_cells)
    local_modes = own * modes + jnp.arange(modes, dtype=jnp.int32)
    strike_modes = jnp.arange(strike_cells, dtype=jnp.int32)
    precise = lax.Precision.HIGH

    def to_rows(planes):
        count = planes.shape[0]
        parts = planes.reshape(count, dip_count, rows, -1)
        parts = jnp.transpose(parts, (1, 3, 0, 2)).reshape(dip_count, -1, count * rows)
        moved = lax.all_to_all(parts, "dip", split_axis=0, concat_axis=0, tiled=True)
        return moved.reshape(dip_cells, count * rows)

    def from_rows(space_rows):
        count = space_rows.shape[1] // rows
        parts = space_rows.reshape(dip_count, -1, count * rows)
        moved = lax.all_to_all(parts, "dip", split_axis=0, concat_axis=0, tiled=True)
        moved = moved.reshape(dip_count, -1, count, rows)
        return jnp.transpose(moved, (2, 0, 3, 1)).reshape(count, row_count, -1)

    def send(space_rows):
        dip_spec = jnp.dot(table, space_rows, precision=precise)
        moved = lax.all_to_all(
            dip_spec, ("strike", "dip"), split_axis=0, concat_axis=0, tiled=True
        )
        return moved.reshape(devices, 2, modes, -1)

    def receive(strike_rows):
        moved = lax.all_to_all(
            strike_rows.reshape(2 * dip_cells, -1),
            ("strike", "dip"),
            split_axis=0,
            concat_axis=0,
            tiled=True,
        )
        return planes_of(jnp.dot(back_table, moved, precision=precise))

    def planes_of(space_rows):
        return [
            space_rows[:, start : start + rows] for start in range(0, space_rows.shape[1], rows)
        ]

    def by_residue(plain):
        lead = plain.shape[:-1]
        return plain.reshape(lead + (rows, devices))

    residue = jnp.arange(devices, dtype=jnp.int32)[:, None, None]
    step = jnp.arange(rows, dtype=jnp.int32)[None, None, :]
    sorted_mixing = all_mixing(
        wave_geometry(local_modes[None, :, None], residue + devices * step, dip_cells, strike_cells)
    )
    reach = jnp.transpose(by_residue(lengths), (2, 0, 1))
    reach = (1 < reach).astype(jnp.float32)
    mixing = jnp.stack(sorted_mixing[0][:3])
    past_mixing = jnp.stack(sorted_mixing[1][:3]) * reach
    open_first, open_past = sorted_mixing[0][3], sorted_mixing[1][3] * reach
    plain_mixing = all_mixing(
        wave_geometry(local_modes[:, None], strike_modes[None, :], dip_cells, strike_cells)
    )

    def sort(plain):
        return jnp.transpose(by_residue(plain), (0, 3, 1, 2))

    def lags(first):
        for offset in range(first, HIST):
            active = (offset < lengths).astype(jnp.float32)
            yield plain_mixing[offset], active, history[offset - first].astype(jnp.float32)

    def past_shear(first):
        strike_sum, dip_sum = 0.0, 0.0
        for (along, cross, across, _), active, source in lags(first):
            strike_sum += (along * source[0] + cross * source[1]) * active
            dip_sum += (cross * source[0] + across * source[1]) * active
        return jnp.stack([sort(strike_sum), sort(dip_sum)])

    def past_open(first):
        summed = 0.0
        for (_, _, _, opening), active, source in lags(first):
            summed += opening * source[2] * active
        return sort(summed)

    def mirror(spectrum):
        flip = np.eye(rows, dtype=np.float32)[::-1]
        apart = jnp.einsum(
            "prim,mn->prin", spectrum[:, 1:][:, ::-1], flip, precision=lax.Precision.HIGHEST
        )
        whole = jnp.einsum(
            "prim,mn->prin",
            spectrum[:, :1],
            np.roll(flip, 1, axis=1),
            precision=lax.Precision.HIGHEST,
        )
        turned = jnp.concatenate([whole, apart], axis=1)
        names = ("strike", "dip")
        rest = lax.ppermute(
            turned[:, :, 1:][:, :, ::-1], names, [(g, devices - 1 - g) for g in range(devices)]
        )
        edge = lax.ppermute(
            turned[:, :, :1], names, [(g, (devices - g) % devices) for g in range(devices)]
        )
        both = jnp.concatenate([edge, rest], axis=2)
        return jnp.stack([both[0], -both[1]])

    slip_rows = to_rows(slip_rate)
    shear = 2 * rows
    arrived = send(slip_rows[:, :shear])
    load = jnp.concatenate(
        [prestress, (direct_effect * normal_stress)[None], state_log[None]]
    )
    load_strike, load_dip, strength, state = planes_of(to_rows(load))
    strike_rows, first_spec = strike_pass(arrived, mixing, past_shear(1), tables, keep=True)

    open_earlier = past_open(1)
    open_add = open_first * (open_earlier + mirror(open_earlier)) + past_open(2)
    open_mix = 2.0 * open_first * open_first + open_past
    (open_strike_rows,) = strike_pass(
        send(slip_rows[:, shear:]), open_mix[None], open_add[None], tables
    )
    (open_force,) = receive(open_strike_rows)

    load_rows = (load_strike, load_dip)
    rates, state = friction_planes(receive(strike_rows), load_rows, strength, state)
    arrived, open_force = lax.optimization_barrier(
        (send(jnp.concatenate(rates, axis=1)), open_force)
    )
    open_rates = from_rows(open_force / radiation)
    (strike_rows,) = strike_pass(
        arrived,
        mixing,
        past_shear(2),
        tables,
        (past_mixing, first_spec),
    )
    rates, state = friction_planes(receive(strike_rows), load_rows, strength, state)
    result, open_rates = lax.optimization_barrier(
        (jnp.concatenate(rates + [state], axis=1), open_rates)
    )
    result = from_rows(result)
    return (jnp.concatenate([result[:2], open_rates]), result[2])


def choose(slip_rate, history, *others):
    devices = lax.axis_size("strike") * lax.axis_size("dip")
    fits = (
        history.shape[4] == devices * LANES
        and history.shape[3] % SUBLANES == 0
        and devices & (devices - 1) == 0
    )
    return (fast_shards if fits else shards)(slip_rate, history, *others)


def solution(mesh):
    return jax.shard_map(
        choose,
        mesh=mesh,
        in_specs=(
            P(None, "strike", "dip"),
            P(None, None, None, ("strike", "dip"), None),
            P(("strike", "dip"), None),
            P(None, "strike", "dip"),
            P("strike", "dip"),
            P("strike", "dip"),
            P("strike", "dip"),
        ),
        out_specs=(P(None, "strike", "dip"), P("strike", "dip")),
        check_vma=False,
    )
```

```python
import functools
import math

import jax
import jax.numpy as jnp
import numpy as np
from jax import lax
from jax.experimental import pallas as pl
from jax.experimental.pallas import tpu as pltpu
from jax.sharding import PartitionSpec as P

HIST = 4
NEWTON = 2


time_step = 0.5
coupling = 0.5
decay_rate = 0.05
shear_speed = 0.6
opening_speed = 1.7
radiation = 0.5
healing = 1.0
slip_length = 2.0
highest = lax.Precision.HIGHEST


def area_sine(ratio):
    return jnp.log(ratio + jnp.sqrt(ratio * ratio + 1.0))


def wave_geometry(dip_modes, strike_modes, dip_cells, strike_cells):
    signed_dip = jnp.where(2 * dip_modes < dip_cells, dip_modes, dip_modes - dip_cells)
    signed_strike = jnp.where(
        2 * strike_modes < strike_cells, strike_modes, strike_modes - strike_cells
    )
    wave_dip = signed_dip.astype(jnp.float32) * (2.0 * math.pi / dip_cells)
    wave_strike = signed_strike.astype(jnp.float32) * (2.0 * math.pi / strike_cells)
    modulus = jnp.sqrt(wave_strike * wave_strike + wave_dip * wave_dip)
    anchor = (signed_dip == 0) & (signed_strike == 0)
    safe_modulus = jnp.where(anchor, 1.0, modulus)
    unit_strike = jnp.where(anchor, 1.0, wave_strike / safe_modulus)
    unit_dip = jnp.where(anchor, 0.0, wave_dip / safe_modulus)
    return (modulus, unit_strike, unit_dip)


def delay_mixing(geometry, delay):
    modulus, unit_strike, unit_dip = geometry
    phase_arg = modulus * (time_step * (delay + 1.0))
    envelope = -coupling * time_step * modulus * jnp.exp(-decay_rate * phase_arg)
    mode_two = envelope * jnp.cos(phase_arg)
    mode_three = envelope * jnp.cos(shear_speed * phase_arg)
    mode_one = envelope * jnp.cos(opening_speed * phase_arg)
    mix_along = unit_strike * unit_strike * mode_two + unit_dip * unit_dip * mode_three
    mix_cross = unit_strike * unit_dip * (mode_two - mode_three)
    mix_across = unit_dip * unit_dip * mode_two + unit_strike * unit_strike * mode_three
    return (mix_along, mix_cross, mix_across, mode_one)


def delay_term(spectrum, mixing, active):
    mix_along, mix_cross, mix_across, mode_one = mixing
    force_strike = (mix_along * spectrum[0] + mix_cross * spectrum[1]) * active
    force_dip = (mix_cross * spectrum[0] + mix_across * spectrum[1]) * active
    force_open = mode_one * spectrum[2] * active
    return jnp.stack([force_strike, force_dip, force_open])


def friction_planes(force_field, prestress, strength, state_log):
    load_strike = prestress[0] + force_field[0]
    load_dip = prestress[1] + force_field[1]
    traction = jnp.sqrt(load_strike * load_strike + load_dip * load_dip)
    factor = 2.0 * radiation * jnp.exp(-state_log)
    estimate = jnp.minimum(traction / strength, area_sine(traction / factor))
    for repeat in range(NEWTON):
        residual = traction - strength * estimate - factor * jnp.sinh(estimate)
        estimate = estimate + residual / (strength + factor * jnp.cosh(estimate))
    slip_speed = (traction - strength * estimate) / radiation
    unit_scale = slip_speed / jnp.maximum(traction, 1.0)
    new_rates = [unit_scale * load_strike, unit_scale * load_dip]
    new_state = state_log + time_step * (healing * jnp.exp(-state_log) - slip_speed / slip_length)
    return (new_rates, new_state)


def friction_step(force_field, prestress, normal_stress, direct_effect, state_log):
    new_rates, new_state = friction_planes(
        force_field, prestress, direct_effect * normal_stress, state_log
    )
    return (jnp.stack(new_rates + [force_field[2] / radiation]), new_state)


def phase_table(first_index, second_index, period):
    turn_count = first_index[:, None] * second_index[None, :] % period
    angle_table = turn_count.astype(jnp.float32) * (2.0 * math.pi / period)
    return (jnp.cos(angle_table), jnp.sin(angle_table))


def contract(pattern, first_operand, second_operand):
    return jnp.einsum(pattern, first_operand, second_operand, precision=highest)


def pair_section(part_real, part_imag, pattern, cos_table, sin_table, sign):
    out_real = contract(pattern, part_real, cos_table) - sign * contract(
        pattern, part_imag, sin_table
    )
    out_imag = contract(pattern, part_imag, cos_table) + sign * contract(
        pattern, part_real, sin_table
    )
    return (out_real, out_imag)


def twist_phase(part_real, part_imag, cos_table, sin_table, sign):
    out_real = cos_table * part_real - sign * sin_table * part_imag
    out_imag = cos_table * part_imag + sign * sin_table * part_real
    return (out_real, out_imag)


def shards(slip_rate, history, lengths, prestress, normal_stress, direct_effect, state_log):
    strike_count = lax.axis_size("strike")
    dip_count = lax.axis_size("dip")
    strike_index = lax.axis_index("strike")
    dip_index = lax.axis_index("dip")
    row_count = slip_rate.shape[1]
    dip_block = slip_rate.shape[2]
    mode_rows = history.shape[3]
    strike_cells = history.shape[4]
    dip_cells = dip_block * dip_count
    unit_modes = dip_count * mode_rows
    quarter_rows = row_count // dip_count
    norm_dip = 1.0 / math.sqrt(dip_cells)
    norm_strike = 1.0 / math.sqrt(strike_cells)
    local_modes = jnp.arange(mode_rows, dtype=jnp.int32)
    dip_modes = (strike_index * dip_count + dip_index) * mode_rows + local_modes
    strike_modes = jnp.arange(strike_cells, dtype=jnp.int32)
    geometry = wave_geometry(dip_modes[:, None], strike_modes[None, :], dip_cells, strike_cells)
    coarse_all = jnp.arange(unit_modes, dtype=jnp.int32)
    coarse_own = dip_index * mode_rows + local_modes
    outer_index = jnp.arange(strike_count, dtype=jnp.int32)
    inner_index = jnp.arange(row_count, dtype=jnp.int32)
    cos_outer, sin_outer = phase_table(outer_index, outer_index, strike_count)
    cos_bend, sin_bend = phase_table(outer_index, inner_index, strike_cells)
    cos_bend = cos_bend * norm_strike
    sin_bend = sin_bend * norm_strike
    cos_inner, sin_inner = phase_table(inner_index, inner_index, row_count)

    def strike_forward(spectral):
        item_count = spectral.shape[0]
        grid_view = spectral.reshape(item_count, 2, mode_rows, strike_count, row_count)
        section_real, section_imag = pair_section(
            grid_view[:, 0], grid_view[:, 1], "ngpr,kp->ngkr", cos_outer, sin_outer, -1.0
        )
        bent_real, bent_imag = twist_phase(section_real, section_imag, cos_bend, sin_bend, -1.0)
        out_real, out_imag = pair_section(
            bent_real, bent_imag, "ngkr,rm->ngmk", cos_inner, sin_inner, -1.0
        )
        return jnp.stack([out_real, out_imag], axis=1).reshape(
            item_count, 2, mode_rows, strike_cells
        )

    def strike_inverse(spectral):
        grid_view = spectral.reshape(3, 2, mode_rows, row_count, strike_count)
        section_real, section_imag = pair_section(
            grid_view[:, 0], grid_view[:, 1], "ngmk,rm->ngrk", cos_inner, sin_inner, 1.0
        )
        bent_real, bent_imag = twist_phase(section_real, section_imag, cos_bend.T, sin_bend.T, 1.0)
        out_real, out_imag = pair_section(
            bent_real, bent_imag, "ngrk,kp->ngpr", cos_outer, sin_outer, 1.0
        )
        return jnp.stack([out_real, out_imag], axis=1).reshape(3, 2, mode_rows, strike_cells)

    def to_modes(space_field):
        gathered = lax.all_gather(space_field, "dip", axis=2, tiled=True)
        cos_first, sin_first = phase_table(coarse_all, coarse_own, unit_modes)
        cos_twist, sin_twist = phase_table(outer_index, coarse_own, dip_cells)
        grid_view = gathered.reshape(3, row_count, unit_modes, strike_count)
        first_real = contract("cxab,au->cxbu", grid_view, cos_first)
        first_imag = -contract("cxab,au->cxbu", grid_view, sin_first)
        bent_real, bent_imag = twist_phase(
            first_real, first_imag, cos_twist * norm_dip, sin_twist * norm_dip, -1.0
        )
        out_real, out_imag = pair_section(
            bent_real, bent_imag, "cxbi,bs->csix", cos_outer, sin_outer, -1.0
        )
        dip_spec = jnp.stack([out_real, out_imag], axis=1).reshape(3, 2, dip_block, row_count)
        return strike_forward(
            lax.all_to_all(dip_spec, "strike", split_axis=2, concat_axis=3, tiled=True)
        )

    def to_space(mode_field):
        mixed_rows = strike_inverse(mode_field)
        sectioned = mixed_rows.reshape(3, 2, mode_rows, strike_count, dip_count * quarter_rows)
        back = lax.all_to_all(
            lax.all_to_all(sectioned, "strike", split_axis=3, concat_axis=2, tiled=True),
            "dip",
            split_axis=4,
            concat_axis=2,
            tiled=True,
        )
        grid_view = back.reshape(3, 2, dip_count, strike_count, mode_rows, quarter_rows)
        cos_last, sin_last = phase_table(coarse_all, coarse_all, unit_modes)
        first_real, first_imag = pair_section(
            grid_view[:, 0], grid_view[:, 1], "cdsix,bs->cxbdi", cos_outer, sin_outer, 1.0
        )
        first_real = first_real.reshape(3, quarter_rows, strike_count, unit_modes)
        first_imag = first_imag.reshape(3, quarter_rows, strike_count, unit_modes)
        cos_twist, sin_twist = phase_table(outer_index, coarse_all, dip_cells)
        bent_real, bent_imag = twist_phase(
            first_real, first_imag, cos_twist * norm_dip, sin_twist * norm_dip, 1.0
        )
        space_part = contract("cxbu,au->cxab", bent_real, cos_last) - contract(
            "cxbu,au->cxab", bent_imag, sin_last
        )
        space_rows = space_part.reshape(3, quarter_rows, dip_cells)
        return lax.all_to_all(space_rows, "dip", split_axis=2, concat_axis=1, tiled=True)

    def transfer(recent):
        recent_count = len(recent)
        summed = jnp.zeros(recent[0].shape, jnp.float32)
        for offset in range(HIST):
            if offset < recent_count:
                source = recent[offset]
            else:
                source = history[offset - recent_count].astype(jnp.float32)
            active = (offset < lengths).astype(jnp.float32)
            summed = summed + delay_term(source, delay_mixing(geometry, float(offset)), active)
        return summed

    first_spec = to_modes(slip_rate)
    force_field = to_space(transfer([first_spec]))
    next_rates, next_state = friction_step(
        force_field, prestress, normal_stress, direct_effect, state_log
    )
    second_spec = to_modes(next_rates)
    force_field = to_space(transfer([second_spec, first_spec]))
    next_rates, next_state = friction_step(
        force_field, prestress, normal_stress, direct_effect, next_state
    )
    return (next_rates, next_state)


LANES = 128
SUBLANES = 8


def turn(part_real, part_imag, count, index, sign):
    index = index % count
    if index == 0:
        return part_real, part_imag
    if 2 * index == count:
        return -part_real, -part_imag
    if 4 * index == count:
        return (-part_imag, part_real) if sign > 0 else (part_imag, -part_real)
    angle = sign * 2.0 * math.pi * index / count
    cosine, sine = math.cos(angle), math.sin(angle)
    if 8 * index == count:
        return (
            cosine * (part_real - part_imag) if sign > 0 else cosine * (part_real + part_imag),
            cosine * (part_imag + part_real) if sign > 0 else cosine * (part_imag - part_real),
        )
    return (
        cosine * part_real - sine * part_imag,
        cosine * part_imag + sine * part_real,
    )


def butterfly(reals, imags, sign):
    count = len(reals)
    if count == 1:
        return reals, imags
    even_real, even_imag = butterfly(reals[0::2], imags[0::2], sign)
    odd_real, odd_imag = butterfly(reals[1::2], imags[1::2], sign)
    top, low = [], []
    for index in range(count // 2):
        bent_real, bent_imag = turn(odd_real[index], odd_imag[index], count, index, sign)
        top.append((even_real[index] + bent_real, even_imag[index] + bent_imag))
        low.append((even_real[index] - bent_real, even_imag[index] - bent_imag))
    both = top + low
    return [item[0] for item in both], [item[1] for item in both]


def split_product(left, high, low):
    left_high = left.astype(jnp.bfloat16)
    left_low = (left - left_high.astype(jnp.float32)).astype(jnp.bfloat16)
    dot = functools.partial(jnp.dot, preferred_element_type=jnp.float32)
    return dot(left_high, high) + (dot(left_low, high) + dot(left_high, low))


def owner_kernel(comps, keep, past, *refs):
    x_ref, mix_ref, add_ref = refs[:3]
    refs = refs[3:]
    if past:
        past_mix_ref, past_ref = refs[:2]
        refs = refs[2:]
    bend_ref, high_ref, low_ref, out_ref = refs[:4]
    line, spec = refs[-2:]
    blocks = x_ref.shape[0]
    rows = blocks * SUBLANES
    width = 2 * LANES
    halves = (slice(0, LANES), slice(LANES, width))
    for comp in range(comps):
        own = slice(comp * LANES, (comp + 1) * LANES)
        reals, imags = butterfly(
            [x_ref[block, 0, :, own] for block in range(blocks)],
            [x_ref[block, 1, :, own] for block in range(blocks)],
            -1,
        )
        for mode in range(blocks):
            cosine = bend_ref[0, pl.ds(mode, 1), :]
            sine = bend_ref[1, pl.ds(mode, 1), :]
            line[comp, mode, :, halves[0]] = reals[mode] * cosine + imags[mode] * sine
            line[comp, mode, :, halves[1]] = imags[mode] * cosine - reals[mode] * sine
        spec[comp] = split_product(
            line[comp].reshape(rows, width), high_ref[0], low_ref[0]
        ).reshape(blocks, SUBLANES, width)
    for part, half in enumerate(halves):
        if comps == 1:
            line[0, :, :, half] = mix_ref[0] * spec[0, :, :, half] + add_ref[0, part]
            continue
        along, across = spec[0, :, :, half], spec[1, :, :, half]
        strike_sum = mix_ref[0] * along + mix_ref[1] * across + add_ref[0, part]
        dip_sum = mix_ref[1] * along + mix_ref[2] * across + add_ref[1, part]
        if past:
            strike_sum += past_mix_ref[0] * past_ref[0, part] + past_mix_ref[1] * past_ref[1, part]
            dip_sum += past_mix_ref[1] * past_ref[0, part] + past_mix_ref[2] * past_ref[1, part]
        line[0, :, :, half] = strike_sum
        line[1, :, :, half] = dip_sum
        if keep:
            refs[4][0, part] = along
            refs[4][1, part] = across
    for comp in range(comps):
        own = slice(comp * LANES, (comp + 1) * LANES)
        spec[comp] = split_product(
            line[comp].reshape(rows, width), high_ref[1], low_ref[1]
        ).reshape(blocks, SUBLANES, width)
        reals, imags = [], []
        for mode in range(blocks):
            cosine = bend_ref[0, pl.ds(mode, 1), :]
            sine = bend_ref[1, pl.ds(mode, 1), :]
            real, imag = spec[comp, mode, :, halves[0]], spec[comp, mode, :, halves[1]]
            reals.append(real * cosine - imag * sine)
            imags.append(imag * cosine + real * sine)
        reals, imags = butterfly(reals, imags, 1)
        for block in range(blocks):
            out_ref[block, 0, :, own] = reals[block]
            out_ref[block, 1, :, own] = imags[block]


def strike_pass(arrived, mixing, addend, tables, past=(), keep=False):
    blocks, _, modes, depth = arrived.shape
    comps = depth // LANES
    wide = pl.BlockSpec((blocks, 2, SUBLANES, depth), lambda tile: (0, 0, tile, 0))
    factors = pl.BlockSpec(
        (mixing.shape[0], blocks, SUBLANES, LANES), lambda tile: (0, 0, tile, 0)
    )
    field = pl.BlockSpec((comps, 2, blocks, SUBLANES, LANES), lambda tile: (0, 0, 0, tile, 0))
    fixed = [
        pl.BlockSpec(item.shape, lambda tile, rank=item.ndim: (0,) * rank) for item in tables
    ]
    out_shape = [jax.ShapeDtypeStruct(arrived.shape, jnp.float32)]
    if keep:
        out_shape.append(jax.ShapeDtypeStruct(addend.shape, jnp.float32))
    return pl.pallas_call(
        functools.partial(owner_kernel, comps, keep, bool(past)),
        grid=(modes // SUBLANES,),
        in_specs=[wide, factors, field] + [factors, field][: len(past)] + fixed,
        out_specs=[wide, field][: len(out_shape)],
        out_shape=out_shape,
        scratch_shapes=[
            pltpu.VMEM((comps, blocks, SUBLANES, 2 * LANES), jnp.float32),
            pltpu.VMEM((comps, blocks, SUBLANES, 2 * LANES), jnp.float32),
        ],
        compiler_params=pltpu.CompilerParams(vmem_limit_bytes=40 * 1024 * 1024),
        cost_estimate=pl.CostEstimate(
            flops=12 * arrived.size * 2 * LANES, bytes_accessed=16 * arrived.size, transcendentals=0
        ),
    )(arrived, mixing, addend, *past, *tables)


def halves_of(table):
    table = table.astype(np.float32)
    high = table.astype(jnp.bfloat16)
    return high, (table - high.astype(np.float32)).astype(jnp.bfloat16)


def strike_tables(blocks, strike_cells):
    first, second = np.arange(blocks)[:, None], np.arange(LANES)[None, :]
    angle = 2.0 * np.pi * (first * second % strike_cells) / strike_cells
    bend = np.stack([np.cos(angle), np.sin(angle)]) / math.sqrt(strike_cells)
    line = np.arange(LANES)
    angle = 2.0 * np.pi * (line[:, None] * line[None, :] % LANES) / LANES
    cosine, sine = np.cos(angle), np.sin(angle)
    forward = np.block([[cosine, -sine], [sine, cosine]])
    inverse = np.block([[cosine, sine], [-sine, cosine]])
    high, low = halves_of(np.stack([forward, inverse]))
    return jnp.asarray(bend, jnp.float32), jnp.asarray(high), jnp.asarray(low)


def dip_tables(devices, dip_cells):
    modes = np.arange(dip_cells)
    angle = 2.0 * np.pi * (modes[:, None] * modes[None, :] % dip_cells) / dip_cells
    pair = np.stack([np.cos(angle), -np.sin(angle)]) / math.sqrt(dip_cells)
    pair = pair.reshape(2, devices, dip_cells // devices, dip_cells).transpose(1, 0, 2, 3)
    pair = pair.reshape(2 * dip_cells, dip_cells)
    return jnp.asarray(pair, jnp.float32), jnp.asarray(pair.T, jnp.float32)


def all_mixing(geometry):
    modulus, unit_strike, unit_dip = geometry
    base = modulus * time_step
    decay = jnp.exp(-decay_rate * base)
    speeds = (1.0, shear_speed, opening_speed)
    one = [jnp.cos(speed * base) for speed in speeds]
    last, now = [1.0, 1.0, 1.0], list(one)
    envelope = -coupling * time_step * modulus
    square_strike, square_dip = unit_strike * unit_strike, unit_dip * unit_dip
    cross = unit_strike * unit_dip
    factors = []
    for _ in range(HIST):
        envelope = envelope * decay
        two, three, opening = (envelope * value for value in now)
        factors.append(
            (
                square_strike * two + square_dip * three,
                cross * (two - three),
                square_dip * two + square_strike * three,
                opening,
            )
        )
        last, now = now, [2.0 * a * b - c for a, b, c in zip(one, now, last)]
    return factors


def fast_shards(slip_rate, history, lengths, prestress, normal_stress, direct_effect, state_log):
    strike_count = lax.axis_size("strike")
    dip_count = lax.axis_size("dip")
    devices = strike_count * dip_count
    row_count = slip_rate.shape[1]
    dip_cells = slip_rate.shape[2] * dip_count
    modes = history.shape[3]
    strike_cells = history.shape[4]
    rows = row_count // dip_count
    own = lax.axis_index("strike") * dip_count + lax.axis_index("dip")
    table, back_table = dip_tables(devices, dip_cells)
    tables = strike_tables(devices, strike_cells)
    local_modes = own * modes + jnp.arange(modes, dtype=jnp.int32)
    strike_modes = jnp.arange(strike_cells, dtype=jnp.int32)
    precise = lax.Precision.HIGH

    def to_rows(planes):
        count = planes.shape[0]
        parts = planes.reshape(count, dip_count, rows, -1)
        parts = jnp.transpose(parts, (1, 3, 0, 2)).reshape(dip_count, -1, count * rows)
        moved = lax.all_to_all(parts, "dip", split_axis=0, concat_axis=0, tiled=True)
        return moved.reshape(dip_cells, count * rows)

    def from_rows(space_rows):
        count = space_rows.shape[1] // rows
        parts = space_rows.reshape(dip_count, -1, count * rows)
        moved = lax.all_to_all(parts, "dip", split_axis=0, concat_axis=0, tiled=True)
        moved = moved.reshape(dip_count, -1, count, rows)
        return jnp.transpose(moved, (2, 0, 3, 1)).reshape(count, row_count, -1)

    def send(space_rows):
        dip_spec = jnp.dot(table, space_rows, precision=precise)
        moved = lax.all_to_all(
            dip_spec, ("strike", "dip"), split_axis=0, concat_axis=0, tiled=True
        )
        return moved.reshape(devices, 2, modes, -1)

    def receive(strike_rows):
        moved = lax.all_to_all(
            strike_rows.reshape(2 * dip_cells, -1),
            ("strike", "dip"),
            split_axis=0,
            concat_axis=0,
            tiled=True,
        )
        return planes_of(jnp.dot(back_table, moved, precision=precise))

    def planes_of(space_rows):
        return [
            space_rows[:, start : start + rows] for start in range(0, space_rows.shape[1], rows)
        ]

    def by_residue(plain):
        lead = plain.shape[:-1]
        return plain.reshape(lead + (rows, devices))

    residue = jnp.arange(devices, dtype=jnp.int32)[:, None, None]
    step = jnp.arange(rows, dtype=jnp.int32)[None, None, :]
    sorted_mixing = all_mixing(
        wave_geometry(local_modes[None, :, None], residue + devices * step, dip_cells, strike_cells)
    )
    reach = jnp.transpose(by_residue(lengths), (2, 0, 1))
    reach = (1 < reach).astype(jnp.float32)
    mixing = jnp.stack(sorted_mixing[0][:3])
    past_mixing = jnp.stack(sorted_mixing[1][:3]) * reach
    open_first, open_past = sorted_mixing[0][3], sorted_mixing[1][3] * reach
    plain_mixing = all_mixing(
        wave_geometry(local_modes[:, None], strike_modes[None, :], dip_cells, strike_cells)
    )

    def sort(plain):
        return jnp.transpose(by_residue(plain), (0, 3, 1, 2))

    def lags(first, older, reached):
        for offset in range(first, HIST):
            active = (offset < reached).astype(jnp.float32)
            yield plain_mixing[offset], active, older[offset - first].astype(jnp.float32)

    def past_shear(first, older, reached):
        strike_sum, dip_sum = 0.0, 0.0
        for (along, cross, across, _), active, source in lags(first, older, reached):
            strike_sum += (along * source[0] + cross * source[1]) * active
            dip_sum += (cross * source[0] + across * source[1]) * active
        return jnp.stack([sort(strike_sum), sort(dip_sum)])

    def past_open(first, older, reached):
        summed = 0.0
        for (_, _, _, opening), active, source in lags(first, older, reached):
            summed += opening * source[2] * active
        return sort(summed)

    def mirror(spectrum):
        flip = np.eye(rows, dtype=np.float32)[::-1]
        apart = jnp.einsum(
            "prim,mn->prin", spectrum[:, 1:][:, ::-1], flip, precision=lax.Precision.HIGHEST
        )
        whole = jnp.einsum(
            "prim,mn->prin",
            spectrum[:, :1],
            np.roll(flip, 1, axis=1),
            precision=lax.Precision.HIGHEST,
        )
        turned = jnp.concatenate([whole, apart], axis=1)
        names = ("strike", "dip")
        rest = lax.ppermute(
            turned[:, :, 1:][:, :, ::-1], names, [(g, devices - 1 - g) for g in range(devices)]
        )
        edge = lax.ppermute(
            turned[:, :, :1], names, [(g, (devices - g) % devices) for g in range(devices)]
        )
        both = jnp.concatenate([edge, rest], axis=2)
        return jnp.stack([both[0], -both[1]])

    slip_rows = to_rows(slip_rate)
    shear = 2 * rows
    arrived = send(slip_rows[:, :shear])
    load = jnp.concatenate(
        [prestress, (direct_effect * normal_stress)[None], state_log[None]]
    )
    load_strike, load_dip, strength, state = planes_of(to_rows(load))
    strike_rows, first_spec = strike_pass(arrived, mixing, past_shear(1, history, lengths), tables, keep=True)

    strike_rows, older, reached = lax.optimization_barrier((strike_rows, history, lengths))
    open_earlier = past_open(1, older, reached)
    open_add = open_first * (open_earlier + mirror(open_earlier)) + past_open(2, older, reached)
    open_mix = 2.0 * open_first * open_first + open_past
    (open_strike_rows,) = strike_pass(
        send(slip_rows[:, shear:]), open_mix[None], open_add[None], tables
    )
    (open_force,) = receive(open_strike_rows)

    load_rows = (load_strike, load_dip)
    rates, state = friction_planes(receive(strike_rows), load_rows, strength, state)
    rates, older, reached = lax.optimization_barrier((rates, older, reached))
    arrived, open_force = lax.optimization_barrier(
        (send(jnp.concatenate(rates, axis=1)), open_force)
    )
    open_rates = from_rows(open_force / radiation)
    (strike_rows,) = strike_pass(
        arrived,
        mixing,
        past_shear(2, older, reached),
        tables,
        (past_mixing, first_spec),
    )
    rates, state = friction_planes(receive(strike_rows), load_rows, strength, state)
    result, open_rates = lax.optimization_barrier(
        (jnp.concatenate(rates + [state], axis=1), open_rates)
    )
    result = from_rows(result)
    return (jnp.concatenate([result[:2], open_rates]), result[2])


def choose(slip_rate, history, *others):
    devices = lax.axis_size("strike") * lax.axis_size("dip")
    fits = (
        history.shape[4] == devices * LANES
        and history.shape[3] % SUBLANES == 0
        and devices & (devices - 1) == 0
    )
    return (fast_shards if fits else shards)(slip_rate, history, *others)


def solution(mesh):
    return jax.shard_map(
        choose,
        mesh=mesh,
        in_specs=(
            P(None, "strike", "dip"),
            P(None, None, None, ("strike", "dip"), None),
            P(("strike", "dip"), None),
            P(None, "strike", "dip"),
            P("strike", "dip"),
            P("strike", "dip"),
            P("strike", "dip"),
        ),
        out_specs=(P(None, "strike", "dip"), P("strike", "dip")),
        check_vma=False,
    )
```
